32 devices in a mesh: parts: 2 (over x), dp: 2 (over core), mp: 8 (over z, y).
Axes of the slice: x: 2, y: 2, z: 4, core: 2. Of those that a mesh axis runs over, the one named last changes fastest.
Arguments:
- hidden_in: bfloat16 [32, 5120], P(('parts', 'dp')), parts along dimension 0, may hold values from -6 to 6
- norm_gain: float32 [5120], replicated, may hold values from 0.1 to 1.9
- w_query: bfloat16 [5120, 8192], P(None, 'mp'), may hold values from -1 to 1
- w_key_value: bfloat16 [5120, 2048], P(None, 'mp'), may hold values from -1 to 1
- w_output: bfloat16 [8192, 5120], P('mp'), may hold values from -0.25 to 0.25
- cache_keys: bfloat16 [32, 512, 1024], P(('parts', 'dp'), 'mp'), parts along dimension 0, may hold values from -200 to 200
- cache_values: bfloat16 [32, 512, 1024], P(('parts', 'dp'), 'mp'), parts along dimension 0, may hold values from -6 to 6
- cache_lengths: int32 [32], P('parts'), parts along dimension 0, may hold values from 64 to 512
- remaining_steps: int32 [32], P('parts'), parts along dimension 0, may hold values from 1 to 4
- move_from: int32 [4], P('parts'), parts along dimension 0, may hold values from 0 to 7, as said below
- move_to: int32 [4], P('parts'), parts along dimension 0, may hold values from 0 to 7, as said below
Outputs:
- hidden_out: bfloat16 [32, 5120], P(('parts', 'dp')), parts along dimension 0
- new_kv: bfloat16 [4, 32, 2048], P(None, ('parts', 'dp'), 'mp'), parts along dimension 1
The draws below stay inside these ranges and needn't reach their ends.
There are 2 independent parts, one for each index of `parts`. The reference program is written for one: setup_inputs(seed, part) draws one part's arguments, and reference() takes and returns one part's arrays. A program takes and returns all parts, laid end to end along the dimension named above; an argument that names none is the same for every part. Nothing has to cross between parts.
Inputs may be any that keep to these rules, and one draw needn't show every extreme that they name: `move_from`: 2 distinct slots. `move_to`: 2 distinct slots.
All inputs are finite; a program needn't handle non-finite values.
Results may differ from the reference program's by a relative error of at most 0.018.
Values may be sent and summed in bfloat16 or wider, within the bound.
No kernel may reach another device: no remote copies, remote signals or barrier semaphores. Data moves between devices by JAX's collectives and lax.ppermute only.
A program may use at most 128 MiB of HBM per device.

```python
import math
from functools import partial
import jax
import jax.numpy as jnp
from jax import lax

D = 5120
QH = 64
KVH = 8
HD = 128
SEQ_GRP = 8
CAP_DEV = 64
STEPS = 4
SEQS = 16
CAP = 512
MOVES = 2
N_MP = 8


def shared_columns(key):
    common = jax.random.normal(jax.random.fold_in(key, 7), (D, KVH * HD), jnp.float32)
    return jnp.clip(common, -4.0, 4.0)


def draw_w_query(key, part):
    common = shared_columns(key)
    key = jax.random.fold_in(key, 61)
    own = jnp.clip(jax.random.normal(key, (D, QH * HD), jnp.float32), -4.0, 4.0)
    spread = jnp.broadcast_to(common.reshape(D, KVH, 1, HD), (D, KVH, QH // KVH, HD)).reshape(D, QH * HD)
    return ((spread + 0.6 * own) * (1.0 / (1.36 ** 0.5 * D ** 0.5))).astype(jnp.bfloat16)


def draw_w_key_value(key, part):
    common = shared_columns(key)
    key = jax.random.fold_in(key, 71)
    value_cols = jnp.clip(jax.random.normal(key, (D, KVH * HD), jnp.float32), -4.0, 4.0)
    return (jnp.concatenate([common, value_cols], axis=1) * (1.0 / D ** 0.5)).astype(jnp.bfloat16)


def plant_spots(key):
    return jax.random.randint(jax.random.fold_in(key, 3), (SEQS,), 0, CAP - 1).astype(jnp.int32)


def draw_cache_keys(key, part):
    key = jax.random.fold_in(key, 11)
    base = 2.0 * jax.random.normal(key, (SEQS, CAP, KVH * HD), jnp.float32)
    base = jnp.clip(base, -12.0, 12.0)
    return base.astype(jnp.bfloat16)


def draw_cache_lengths(key, part):
    spots = plant_spots(key)
    key = jax.random.fold_in(key, 21)
    first_key, second_key = jax.random.split(key)
    lengths = jax.random.randint(first_key, (SEQS,), CAP // 8, CAP + 1)
    lengths = jnp.maximum(lengths, spots + 2)
    chosen = jax.random.permutation(second_key, SEQS)[:2]
    lengths = lengths.at[chosen[0]].set(CAP)
    lengths = lengths.at[chosen[1]].set(CAP // 8)
    return lengths.astype(jnp.int32)


def draw_remaining_steps(key, part):
    key = jax.random.fold_in(key, 31)
    first_key, second_key = jax.random.split(key)
    counts = jax.random.randint(first_key, (SEQS,), 1, STEPS + 1)
    spots = jax.random.permutation(second_key, SEQS)[:2]
    counts = counts.at[spots[0]].set(STEPS)
    counts = counts.at[spots[1]].set(1)
    return counts.astype(jnp.int32)


def pick_slots(key):
    first_key, second_key = jax.random.split(key)
    inner = jax.random.permutation(first_key, SEQ_GRP - 2)[:MOVES - 2] + 1
    chosen = jnp.concatenate([jnp.array([0, SEQ_GRP - 1], jnp.int32), inner.astype(jnp.int32)])
    return jax.random.permutation(second_key, chosen).astype(jnp.int32)


def draw_move_from(key, part):
    key = jax.random.fold_in(key, 41)
    return pick_slots(key)


def draw_move_to(key, part):
    key = jax.random.fold_in(key, 51)
    return pick_slots(key)


def level_of(key, dims, shards, least, high):
    factor_of, own = 1.0, jax.random.fold_in(key, 6)
    for dim, shards_of in shards:
        heights = jnp.exp(jax.random.uniform(jax.random.fold_in(own, dim), (shards_of,), jnp.float32, least / len(shards), high / len(shards)))
        factor_of = factor_of * jnp.repeat(heights, dims[dim] // shards_of).reshape([-1 if axis == dim else 1 for axis in range(len(dims))])
    return factor_of


def normal_values(own_key, shape, scale, bound, shards=(), held_as=jnp.bfloat16):
    entries = jax.random.normal(own_key, shape, jnp.float32) * scale
    if len(shards) > 0:
        entries = level_of(own_key, shape, shards, -0.22, 0.18) * entries
    return jnp.clip(entries, min=-bound, max=bound).astype(held_as)


def setup_inputs(seed: int = 0, part: int = 0) -> dict:
    arg_keys = jax.random.split(jax.random.key(seed), 12)
    part_keys = jax.random.split(jax.random.fold_in(arg_keys[11], part), 12)
    hidden_in = normal_values(part_keys[0], (SEQS, D), 1.0, 6.0, ((0, 2),))
    norm_gain = jnp.clip(1.0 + 0.18 * jax.random.normal(arg_keys[1], (D,), jnp.float32), 0.1, 1.9)
    w_query = draw_w_query(jax.random.fold_in(arg_keys[11], 71), part)
    w_key_value = draw_w_key_value(jax.random.fold_in(arg_keys[11], 71), part)
    w_output = normal_values(arg_keys[4], (QH * HD, D), (QH * HD // 16) ** -0.5, 0.25, ((0, 8),))
    cache_keys = draw_cache_keys(jax.random.fold_in(jax.random.fold_in(arg_keys[11], part), 71), part)
    cache_values = normal_values(part_keys[6], (SEQS, CAP, KVH * HD), 1.0, 6.0, ((0, 2), (1, 8)))
    cache_lengths = draw_cache_lengths(jax.random.fold_in(jax.random.fold_in(arg_keys[11], part), 71), part)
    remaining_steps = draw_remaining_steps(jax.random.fold_in(jax.random.fold_in(arg_keys[11], part), 71), part)
    move_from = draw_move_from(jax.random.fold_in(jax.random.fold_in(arg_keys[11], part), 71), part)
    move_to = draw_move_to(jax.random.fold_in(jax.random.fold_in(arg_keys[11], part), 71), part)
    return {"hidden_in": hidden_in, "norm_gain": norm_gain, "w_query": w_query, "w_key_value": w_key_value, "w_output": w_output, "cache_keys": cache_keys, "cache_values": cache_values, "cache_lengths": cache_lengths, "remaining_steps": remaining_steps, "move_from": move_from, "move_to": move_to}


rope_base = 1000000.0
norm_eps = 1e-06

def root_norm(values):
    return values * lax.rsqrt(lax.optimization_barrier(jnp.mean(values * values, axis=-1, keepdims=True)) + norm_eps)

def rotate(values, positions):
    half_width = values.shape[-1] // 2
    frequency = rope_base ** (-jnp.arange(half_width).astype(jnp.float32) * 2.0 / values.shape[-1])
    angles = positions.astype(jnp.float32)[:, None] * frequency[None, :]
    cosine = jnp.cos(angles)[:, None, :]
    sine_part = jnp.sin(angles)[:, None, :]
    first_half = values[..., :half_width]
    second_half = values[..., half_width:]
    return jnp.concatenate([first_half * cosine - second_half * sine_part, second_half * cosine + first_half * sine_part], axis=-1)

def attend_one(inputs, step_index):
    query_row, key_rows, value_rows, length, fresh_keys, fresh_values = inputs
    group_size = QH // KVH
    score_scale = 1.0 / math.sqrt(HD)
    grouped = query_row.astype(jnp.float32).reshape(KVH, group_size, HD)
    key_blocks = key_rows.astype(jnp.float32).reshape(N_MP, CAP_DEV, KVH, HD)
    value_blocks = value_rows.astype(jnp.float32).reshape(N_MP, CAP_DEV, KVH, HD)
    scores = jnp.einsum('kgd,bpkd->kgbp', grouped, key_blocks) * score_scale
    valid_mask = jnp.arange(CAP).reshape(N_MP, CAP_DEV) < length
    block_max = lax.optimization_barrier(jnp.max(jnp.where(valid_mask, scores, -1e+30), axis=-1))
    weights = jnp.where(valid_mask, jnp.exp(scores - block_max[..., None]), 0.0).astype(jnp.bfloat16)
    numerator = jnp.einsum('kgbp,bpkd->kgbd', weights.astype(jnp.float32), value_blocks)
    denominator = lax.optimization_barrier(jnp.sum(weights.astype(jnp.float32), axis=-1))
    fresh_scores = jnp.einsum('kgd,tkd->kgt', grouped, fresh_keys.astype(jnp.float32)) * score_scale
    fresh_mask = jnp.arange(STEPS) <= step_index
    fresh_max = lax.optimization_barrier(jnp.max(jnp.where(fresh_mask, fresh_scores, -1e+30), axis=-1))
    fresh_weights = jnp.where(fresh_mask, jnp.exp(fresh_scores - fresh_max[..., None]), 0.0).astype(jnp.bfloat16)
    fresh_num = jnp.einsum('kgt,tkd->kgd', fresh_weights.astype(jnp.float32), fresh_values.astype(jnp.float32))
    fresh_den = lax.optimization_barrier(jnp.sum(fresh_weights.astype(jnp.float32), axis=-1))
    top_score = jnp.maximum(lax.optimization_barrier(jnp.max(block_max, axis=-1)), fresh_max)
    block_scale = jnp.exp(block_max - top_score[..., None])
    fresh_scale = jnp.exp(fresh_max - top_score)
    weighted = lax.optimization_barrier(jnp.sum(block_scale[..., None] * numerator, axis=2)) + fresh_scale[..., None] * fresh_num
    mass_sum = lax.optimization_barrier(jnp.sum(block_scale * denominator, axis=-1)) + fresh_scale * fresh_den
    return (weighted / mass_sum[..., None]).reshape(QH * HD)

def reference(hidden_in, norm_gain, w_query, w_key_value, w_output, cache_keys, cache_values, cache_lengths, remaining_steps, move_from, move_to):
    hidden = hidden_in
    fresh_keys = jnp.zeros((SEQS, STEPS, KVH, HD), jnp.bfloat16)
    fresh_values = jnp.zeros((SEQS, STEPS, KVH, HD), jnp.bfloat16)
    kv_rows = []
    for step_index in range(STEPS):
        active = remaining_steps > step_index
        positions = cache_lengths + step_index
        hidden_float = hidden.astype(jnp.float32)
        normed = (root_norm(hidden_float) * norm_gain).astype(jnp.bfloat16)
        projected = jnp.dot(normed, w_query, preferred_element_type=jnp.float32).reshape(SEQS, QH, HD)
        queries = rotate(root_norm(projected), positions).astype(jnp.bfloat16)
        raw_proj = jnp.dot(normed, w_key_value, preferred_element_type=jnp.float32).astype(jnp.bfloat16)
        key_part = raw_proj[:, :KVH * HD].astype(jnp.float32).reshape(SEQS, KVH, HD)
        new_keys = rotate(root_norm(key_part), positions).astype(jnp.bfloat16)
        new_values = raw_proj[:, KVH * HD:].reshape(SEQS, KVH, HD)
        new_keys = jnp.where(active[:, None, None], new_keys, jnp.zeros_like(new_keys))
        new_values = jnp.where(active[:, None, None], new_values, jnp.zeros_like(new_values))
        fresh_keys = fresh_keys.at[:, step_index].set(new_keys)
        fresh_values = fresh_values.at[:, step_index].set(new_values)
        kv_rows.append(jnp.concatenate([new_keys.reshape(SEQS, KVH * HD), new_values.reshape(SEQS, KVH * HD)], axis=-1))
        attended = lax.map(partial(attend_one, step_index=step_index), (queries, cache_keys, cache_values, cache_lengths, fresh_keys, fresh_values)).astype(jnp.bfloat16)
        update = jnp.dot(attended, w_output, preferred_element_type=jnp.float32)
        hidden = jnp.where(active[:, None], hidden_float + update, hidden_float).astype(jnp.bfloat16)
    new_order = jnp.arange(SEQS).astype(jnp.int32)
    new_order = new_order.at[move_from].set(move_to + SEQ_GRP)
    new_order = new_order.at[move_to + SEQ_GRP].set(move_from)
    return (hidden[new_order], jnp.stack(kv_rows)[:, new_order])
```

```python
import functools
import math

import jax
import jax.numpy as jnp
from jax import lax
from jax.experimental import pallas as pl
from jax.experimental.pallas import tpu as pltpu
from jax.sharding import PartitionSpec as P

HD = 128
STEPS = 4
KERNEL_VMEM = 18 * 2**20


rope_base = 1000000.0
norm_eps = 1e-06

in_vmem = pl.BlockSpec(memory_space=pltpu.VMEM)
in_smem = pl.BlockSpec(memory_space=pltpu.SMEM)
in_place = pl.BlockSpec(memory_space=pl.ANY)


def exchange(block, axis, mask):
    count = lax.axis_size(axis)
    return lax.ppermute(block, axis, [(low, low ^ mask) for low in range(count)])


def root_norm(values):
    return values * lax.rsqrt(jnp.mean(values * values, axis=-1, keepdims=True) + norm_eps)


def turn(values, cosine, sine):
    return values * cosine + pltpu.roll(values, values.shape[-1] // 2, 1) * sine


def pack_kernel(index_ref, keys_ref, values_ref, *rest):
    outs, sems = rest[:-1], rest[-1]
    me = index_ref[0]
    copies = []
    for step, out in enumerate(outs):
        head = pl.multiple_of((me ^ step) * HD, HD)
        for which, source in enumerate((keys_ref, values_ref)):
            copies.append(
                pltpu.make_async_copy(
                    source.at[:, :, pl.ds(head, HD)], out.at[which], sems.at[2 * step + which]
                )
            )
    for copy in copies:
        copy.start()
    for copy in copies:
        copy.wait()


def norm_kernel(has_update, *refs):
    if has_update:
        hidden_ref, first_ref, second_ref, active_before_ref, *refs = refs
    else:
        hidden_ref, *refs = refs
    gain_ref, w_ref, hidden_out, normed_out, raw_out = refs
    hidden = hidden_ref[...].astype(jnp.float32)
    if has_update:
        update = first_ref[...].astype(jnp.float32) + second_ref[...].astype(jnp.float32)
        keep = active_before_ref[:, :1] > 0.0
        hidden = jnp.where(keep, hidden + update, hidden).astype(jnp.bfloat16)
        hidden_out[...] = hidden
        hidden = hidden.astype(jnp.float32)
    else:
        hidden_out[...] = hidden_ref[...]
    normed = (root_norm(hidden) * gain_ref[...]).astype(jnp.bfloat16)
    normed_out[...] = normed
    raw_out[...] = jnp.dot(normed, w_ref[...], preferred_element_type=jnp.float32).astype(
        jnp.bfloat16
    )


def key_kernel(index_ref, raw_ref, cos_ref, sin_ref, active_ref, both_out, a_out, b_out):
    is_key = index_ref[1] == 1
    live = active_ref[...] > 0.0
    done = []
    for head in range(2):
        raw = raw_ref[:, head * HD : (head + 1) * HD].astype(jnp.float32)
        turned = turn(root_norm(raw), cos_ref[...], sin_ref[...])
        chosen = jnp.where(is_key, turned, raw)
        done.append(jnp.where(live, chosen, 0.0).astype(jnp.bfloat16))
        both_out[:, head * HD : (head + 1) * HD] = done[head]
    a_out[...] = jnp.where(is_key, done[0], done[1])
    b_out[...] = jnp.where(is_key, done[1], done[0])


def query_kernel(
    block_count,
    lengths_ref,
    normed_ref,
    w_ref,
    cos_ref,
    sin_ref,
    places_ref,
    *rest,
):
    caches, rest = rest[:block_count], rest[block_count:]
    query_out, num_out, max_out, den_out = rest
    seq_count = normed_ref.shape[0]
    heads = w_ref.shape[1] // HD
    projected = jnp.dot(normed_ref[...], w_ref[...], preferred_element_type=jnp.float32)
    for head in range(heads):
        piece = projected[:, head * HD : (head + 1) * HD]
        turned = turn(root_norm(piece), cos_ref[...], sin_ref[...])
        query_out[head] = turned.astype(jnp.bfloat16).astype(jnp.float32)
    places = places_ref[...]

    def rows(which, seq):
        return jnp.concatenate(
            [ref[which, seq] if ref.ndim == 4 else ref[:, which, seq].reshape(-1, HD) for ref in caches],
            axis=0,
        )

    for seq in range(seq_count):
        query = query_out[:, seq, :].astype(jnp.bfloat16)
        scores = lax.dot_general(
            query, rows(0, seq), (((1,), (1,)), ((), ())), preferred_element_type=jnp.float32
        ) * (1.0 / math.sqrt(HD))
        valid = places < lengths_ref[seq]
        top = jnp.max(jnp.where(valid, scores, -1e30), axis=-1, keepdims=True)
        weights = jnp.where(valid, jnp.exp(scores - top), 0.0).astype(jnp.bfloat16)
        mass = jnp.sum(weights.astype(jnp.float32), axis=-1, keepdims=True)
        num_out[:, seq, :] = jnp.dot(weights, rows(1, seq), preferred_element_type=jnp.float32)
        max_out[:, seq, :] = jnp.broadcast_to(top, (heads, HD))
        den_out[:, seq, :] = jnp.broadcast_to(mass, (heads, HD))


def output_kernel(fresh_count, query_ref, num_ref, max_ref, den_ref, w_ref, *rest):
    fresh, out_ref = rest[:-1], rest[-1]
    heads = query_ref.shape[0]
    keys = [ref[...].astype(jnp.float32) for ref in fresh[:fresh_count]]
    values = [ref[...].astype(jnp.float32) for ref in fresh[fresh_count:]]
    attended = []
    for head in range(heads):
        query = query_ref[head]
        scores = [
            jnp.sum(query * key, axis=-1, keepdims=True) * (1.0 / math.sqrt(HD)) for key in keys
        ]
        top_old = max_ref[head]
        top = functools.reduce(jnp.maximum, scores, top_old)
        scale = jnp.exp(top_old - top)
        num = scale * num_ref[head]
        den = scale * den_ref[head]
        for score, value in zip(scores, values):
            weight = jnp.exp(score - top).astype(jnp.bfloat16).astype(jnp.float32)
            num = num + weight * value
            den = den + weight
        attended.append((num / den).astype(jnp.bfloat16))
    out_ref[...] = jnp.dot(
        jnp.concatenate(attended, axis=1), w_ref[...], preferred_element_type=jnp.float32
    ).astype(jnp.bfloat16)


def sum_rounds(part, axis):
    masks = [1 << bit for bit in range(lax.axis_size(axis).bit_length() - 1)]
    rounds = [masks[at : at + 2] for at in range(0, len(masks), 2)]
    if len(rounds[-1]) == 2:
        rounds = rounds[:-1] + [rounds[-1][:1], rounds[-1][1:]]
    for masks_now in rounds[:-1]:
        if len(masks_now) == 1:
            total = part.astype(jnp.float32) + exchange(part, axis, masks_now[0]).astype(jnp.float32)
        else:
            low, high = masks_now
            near = exchange(part, axis, low)
            far = exchange(part, axis, high)
            both = exchange(part, axis, low | high)
            total = (part.astype(jnp.float32) + near.astype(jnp.float32)) + (
                far.astype(jnp.float32) + both.astype(jnp.float32)
            )
        part = total.astype(jnp.bfloat16)
    return part, exchange(part, axis, rounds[-1][0])


def trade(own, other, slots_here, slots_there, axis):
    rows = jnp.arange(own.shape[axis])
    hits = slots_here[None, :] == rows[:, None]
    picks = jnp.any(
        hits[:, :, None] & (slots_there[None, :, None] == rows[None, None, :]), axis=1
    ).astype(own.dtype)
    moved = jnp.tensordot(picks, other, axes=((1,), (axis,)), preferred_element_type=jnp.float32)
    moved = jnp.moveaxis(moved, 0, axis).astype(own.dtype)
    shape = [1] * own.ndim
    shape[axis] = -1
    return jnp.where(jnp.any(hits, axis=1).reshape(shape), moved, own)


def per_device(
    hidden_in,
    norm_gain,
    w_query,
    w_key_value,
    w_output,
    cache_keys,
    cache_values,
    cache_lengths,
    remaining_steps,
    move_from,
    move_to,
):
    bf16, f32 = jnp.bfloat16, jnp.float32
    seq_count, width = hidden_in.shape
    model_size = lax.axis_size("mp")
    model_index = lax.axis_index("mp")
    group_index = lax.axis_index("dp")
    heads_here = w_query.shape[1] // HD
    kv_width = cache_keys.shape[2]
    kv_heads = kv_width // HD
    block_len = cache_keys.shape[1]
    col_width = w_key_value.shape[1]
    one_head_each = model_size == kv_heads and col_width == 2 * HD

    lengths = lax.dynamic_slice_in_dim(cache_lengths, group_index * seq_count, seq_count)
    remaining = lax.dynamic_slice_in_dim(remaining_steps, group_index * seq_count, seq_count)
    own_head = model_index * kv_heads // model_size
    flags = jnp.stack([model_index, (model_index < model_size // 2).astype(jnp.int32)])

    if one_head_each:
        shape = jax.ShapeDtypeStruct((2, seq_count, block_len, HD), bf16)
        packed = pl.pallas_call(
            pack_kernel,
            out_shape=[shape] * model_size,
            in_specs=[in_smem, in_place, in_place],
            out_specs=[in_place] * model_size,
            scratch_shapes=[pltpu.SemaphoreType.DMA((2 * model_size,))],
        )(flags, cache_keys, cache_values)
        order = sorted(range(1, model_size), key=lambda mask: mask < model_size // 2)
        blocks = {0: packed[0]}
        for mask in order:
            blocks[mask] = exchange(packed[mask], "mp", mask)
        caches = [blocks[mask] for mask in range(model_size)]
        block_index = jnp.stack([model_index ^ mask for mask in range(model_size)])
    else:
        both = jnp.stack([cache_keys, cache_values]).reshape(
            2, seq_count, block_len, kv_heads, HD
        )
        to_all = jnp.repeat(jnp.moveaxis(both, 3, 0), model_size // kv_heads, axis=0)
        caches = [lax.all_to_all(to_all, "mp", 0, 0, tiled=True)]
        block_index = jnp.arange(model_size)
    places = (block_index[:, None] * block_len + jnp.arange(block_len)[None, :]).reshape(1, -1)

    half = HD // 2
    frequency = rope_base ** (-jnp.arange(half).astype(f32) * 2.0 / HD)
    cosines, sines, actives = [], [], []
    for step_index in range(STEPS):
        angles = (lengths + step_index).astype(f32)[:, None] * frequency[None, :]
        cosines.append(jnp.concatenate([jnp.cos(angles)] * 2, axis=1))
        sine = jnp.sin(angles)
        sines.append(jnp.concatenate([-sine, sine], axis=1))
        actives.append(
            jnp.broadcast_to((remaining > step_index).astype(f32)[:, None], (seq_count, HD))
        )

    gain = norm_gain.reshape(1, width)
    hidden = hidden_in
    terms = ()
    fresh_keys, fresh_values, kv_outputs = [], [], []
    row_f32 = jax.ShapeDtypeStruct((heads_here, seq_count, HD), f32)
    row_bf16 = jax.ShapeDtypeStruct((seq_count, width), bf16)
    for step_index in range(STEPS):
        hidden, normed, raw = pl.pallas_call(
            functools.partial(norm_kernel, step_index > 0),
            out_shape=[row_bf16, row_bf16, jax.ShapeDtypeStruct((seq_count, col_width), bf16)],
            in_specs=[in_vmem] * (6 if step_index > 0 else 3),
            out_specs=[in_vmem] * 3,
            compiler_params=pltpu.CompilerParams(vmem_limit_bytes=KERNEL_VMEM),
        )(
            hidden,
            *terms,
            *([actives[step_index - 1]] if step_index > 0 else []),
            gain,
            w_key_value,
        )
        if one_head_each:
            head_row = jax.ShapeDtypeStruct((seq_count, HD), bf16)
            both, sent_a, sent_b = pl.pallas_call(
                key_kernel,
                out_shape=[jax.ShapeDtypeStruct((seq_count, col_width), bf16), head_row, head_row],
                in_specs=[in_smem] + [in_vmem] * 4,
                out_specs=[in_vmem] * 3,
            )(flags, raw, cosines[step_index], sines[step_index], actives[step_index])
            kv_outputs.append(both)
            pairs = model_size // 2
            got_a = lax.ppermute(
                sent_a,
                "mp",
                [(low, 2 * low) for low in range(pairs)]
                + [(pairs + low, 2 * low + 1) for low in range(pairs)],
            )
            got_b = lax.ppermute(
                sent_b,
                "mp",
                [(low, 2 * low + 1) for low in range(pairs)]
                + [(pairs + low, 2 * low) for low in range(pairs)],
            )
            even = model_index % 2 == 0
            new_key = jnp.where(even, got_a, got_b)
            new_value = jnp.where(even, got_b, got_a)
        else:
            raw_full = lax.all_gather(raw, "mp", axis=1, tiled=True)
            key_part = raw_full[:, :kv_width].astype(f32).reshape(seq_count, kv_heads, HD)
            key_part = root_norm(key_part)
            swapped = jnp.concatenate([key_part[..., half:], key_part[..., :half]], axis=-1)
            new_keys = (
                key_part * cosines[step_index][:, None, :] + swapped * sines[step_index][:, None, :]
            ).astype(bf16)
            new_values = raw_full[:, kv_width:].reshape(seq_count, kv_heads, HD)
            live = (remaining > step_index)[:, None, None]
            new_kv = jnp.where(live, jnp.concatenate([new_keys, new_values], axis=1), 0)
            kv_outputs.append(
                lax.dynamic_slice_in_dim(
                    new_kv.reshape(seq_count, 2 * kv_width), model_index * col_width, col_width, 1
                )
            )
            new_key = lax.dynamic_index_in_dim(new_kv, own_head, 1, False)
            new_value = lax.dynamic_index_in_dim(new_kv, kv_heads + own_head, 1, False)
        fresh_keys.append(new_key)
        fresh_values.append(new_value)
        queries, num, top, den = pl.pallas_call(
            functools.partial(query_kernel, len(caches)),
            out_shape=[row_f32] * 4,
            in_specs=[in_smem] + [in_vmem] * (5 + len(caches)),
            out_specs=[in_vmem] * 4,
            cost_estimate=pl.CostEstimate(
                flops=2 * seq_count * width * heads_here * HD,
                bytes_accessed=2 * width * heads_here * HD,
                transcendentals=0,
            ),
            compiler_params=pltpu.CompilerParams(vmem_limit_bytes=KERNEL_VMEM),
        )(lengths, normed, w_query, cosines[step_index], sines[step_index], places, *caches)
        part = pl.pallas_call(
            functools.partial(output_kernel, step_index + 1),
            out_shape=row_bf16,
            in_specs=[in_vmem] * (5 + 2 * (step_index + 1)),
            out_specs=in_vmem,
            compiler_params=pltpu.CompilerParams(vmem_limit_bytes=KERNEL_VMEM),
        )(queries, num, top, den, w_output, *fresh_keys, *fresh_values)
        terms = sum_rounds(part, "mp")
    update = terms[0].astype(f32) + terms[1].astype(f32)
    hidden_float = hidden.astype(f32)
    hidden = jnp.where(
        (remaining > STEPS - 1)[:, None], hidden_float + update, hidden_float
    ).astype(bf16)
    kv_local = jnp.stack(kv_outputs)

    slots_here = jnp.where(group_index == 0, move_from, move_to)
    slots_there = jnp.where(group_index == 0, move_to, move_from)
    other_kv = exchange(kv_local, "dp", 1)
    other_hidden = exchange(hidden, "dp", 1)
    return (
        trade(hidden, other_hidden, slots_here, slots_there, 0),
        trade(kv_local, other_kv, slots_here, slots_there, 1),
    )


def solution(mesh):
    placed = (
        P(("parts", "dp"), None),
        P(),
        P(None, "mp"),
        P(None, "mp"),
        P("mp", None),
        P(("parts", "dp"), "mp", None),
        P(("parts", "dp"), "mp", None),
        P("parts"),
        P("parts"),
        P("parts"),
        P("parts"),
    )
    return jax.shard_map(
        per_device,
        mesh=mesh,
        in_specs=placed,
        out_specs=(P(("parts", "dp"), None), P(None, ("parts", "dp"), "mp")),
        check_vma=False,
    )
```

```python
import functools
import math

import jax
import jax.numpy as jnp
from jax import lax
from jax.experimental import pallas as pl
from jax.experimental.pallas import tpu as pltpu
from jax.sharding import PartitionSpec as P

HD = 128
STEPS = 4
KERNEL_VMEM = 18 * 2**20
SMALL_VMEM = 6 * 2**20


rope_base = 1000000.0
norm_eps = 1e-06

in_vmem = pl.BlockSpec(memory_space=pltpu.VMEM)
in_smem = pl.BlockSpec(memory_space=pltpu.SMEM)


def exchange(block, axis, mask):
    count = lax.axis_size(axis)
    return lax.ppermute(block, axis, [(low, low ^ mask) for low in range(count)])


def root_norm(values):
    return values * lax.rsqrt(jnp.mean(values * values, axis=-1, keepdims=True) + norm_eps)


def turn(values, cosine, sine):
    return values * cosine + pltpu.roll(values, values.shape[-1] // 2, 1) * sine


def pack_kernel(masks, index_ref, keys_ref, values_ref, *outs):
    me = index_ref[0]
    for mask, out in zip(masks, outs):
        head = pl.multiple_of((me ^ mask) * HD, HD)
        out[0] = keys_ref[:, :, pl.ds(head, HD)]
        out[1] = values_ref[:, :, pl.ds(head, HD)]


def norm_kernel(step, split_heads, index_ref, tables_ref, remaining_ref, gain_ref, w_ref, *refs):
    if step > 0:
        hidden_ref, first_ref, second_ref, *refs = refs
    else:
        hidden_ref, *refs = refs
    hidden = hidden_ref[...].astype(jnp.float32)
    if step > 0:
        hidden_out, *refs = refs
        update = first_ref[...].astype(jnp.float32) + second_ref[...].astype(jnp.float32)
        keep = remaining_ref[:, :1] > step - 1
        hidden = jnp.where(keep, hidden + update, hidden).astype(jnp.bfloat16)
        hidden_out[...] = hidden
        hidden = hidden.astype(jnp.float32)
    normed = (root_norm(hidden) * gain_ref[...]).astype(jnp.bfloat16)
    normed_out, raw_out, *refs = refs
    normed_out[...] = normed
    raw = jnp.dot(normed, w_ref[...], preferred_element_type=jnp.float32).astype(jnp.bfloat16)
    if not split_heads:
        raw_out[...] = raw
        return
    is_key = index_ref[1] == 1
    live = remaining_ref[...] > step
    done = []
    for head in range(2):
        piece = raw[:, head * HD : (head + 1) * HD].astype(jnp.float32)
        turned = turn(root_norm(piece), tables_ref[step, 0], tables_ref[step, 1])
        chosen = jnp.where(is_key, turned, piece)
        done.append(jnp.where(live, chosen, 0.0))
        raw_out[:, head * HD : (head + 1) * HD] = done[head].astype(jnp.bfloat16)
    a_out, b_out = refs
    a_out[...] = jnp.where(is_key, done[0], done[1]).astype(jnp.bfloat16)
    b_out[...] = jnp.where(is_key, done[1], done[0]).astype(jnp.bfloat16)


def query_kernel(step, masks, index_ref, lengths_ref, tables_ref, normed_ref, w_ref, *rest):
    caches, rest = rest[: len(masks)], rest[len(masks) :]
    query_out, num_out, max_out, den_out = rest
    caches = [cache for _, cache in sorted(zip(masks, caches), key=lambda pair: pair[0])]
    seq_count = normed_ref.shape[0]
    heads = w_ref.shape[1] // HD
    projected = jnp.dot(normed_ref[...], w_ref[...], preferred_element_type=jnp.float32)
    for head in range(heads):
        piece = projected[:, head * HD : (head + 1) * HD]
        turned = turn(root_norm(piece), tables_ref[step, 0], tables_ref[step, 1])
        query_out[head] = turned.astype(jnp.bfloat16).astype(jnp.float32)

    def rows(which, seq):
        return jnp.concatenate(
            [
                ref[which, seq] if ref.ndim == 4 else ref[:, which, seq].reshape(-1, HD)
                for ref in caches
            ],
            axis=0,
        )

    scores = [
        lax.dot_general(
            query_out[:, seq, :].astype(jnp.bfloat16),
            rows(0, seq),
            (((1,), (1,)), ((), ())),
            preferred_element_type=jnp.float32,
        )
        * (1.0 / math.sqrt(HD))
        for seq in range(seq_count)
    ]
    places = lax.broadcasted_iota(jnp.int32, scores[0].shape, 1) ^ index_ref[3]
    valids = [places < lengths_ref[seq] for seq in range(seq_count)]
    tops = [
        jnp.max(jnp.where(valid, score, -1e30), axis=-1, keepdims=True)
        for valid, score in zip(valids, scores)
    ]
    weights = [
        jnp.where(valid, jnp.exp(score - top), 0.0).astype(jnp.bfloat16)
        for valid, score, top in zip(valids, scores, tops)
    ]
    for seq in range(seq_count):
        num_out[:, seq, :] = jnp.dot(
            weights[seq], rows(1, seq), preferred_element_type=jnp.float32
        )
        mass = jnp.sum(weights[seq].astype(jnp.float32), axis=-1, keepdims=True)
        max_out[:, seq, :] = jnp.broadcast_to(tops[seq], (heads, HD))
        den_out[:, seq, :] = jnp.broadcast_to(mass, (heads, HD))


def output_kernel(index_ref, query_ref, num_ref, max_ref, den_ref, w_ref, *rest):
    fresh, out_ref = rest[:-1], rest[-1]
    heads = query_ref.shape[0]
    key_first = index_ref[2] == 1
    keys, values = [], []
    for one_ref, other_ref in zip(fresh[0::2], fresh[1::2]):
        one, other = one_ref[...].astype(jnp.float32), other_ref[...].astype(jnp.float32)
        keys.append(jnp.where(key_first, one, other))
        values.append(jnp.where(key_first, other, one))
    attended = []
    for head in range(heads):
        query = query_ref[head]
        scores = [
            jnp.sum(query * key, axis=-1, keepdims=True) * (1.0 / math.sqrt(HD)) for key in keys
        ]
        top_old = max_ref[head]
        top = functools.reduce(jnp.maximum, scores, top_old)
        scale = jnp.exp(top_old - top)
        num = scale * num_ref[head]
        den = scale * den_ref[head]
        for score, value in zip(scores, values):
            weight = jnp.exp(score - top).astype(jnp.bfloat16).astype(jnp.float32)
            num = num + weight * value
            den = den + weight
        attended.append((num / den).astype(jnp.bfloat16))
    out_ref[...] = jnp.dot(
        jnp.concatenate(attended, axis=1), w_ref[...], preferred_element_type=jnp.float32
    ).astype(jnp.bfloat16)


def sum_rounds(part, axis):
    masks = [1 << bit for bit in range(lax.axis_size(axis).bit_length() - 1)]
    rounds = [masks[at : at + 2] for at in range(0, len(masks), 2)]
    if len(rounds[-1]) == 2:
        rounds = rounds[:-1] + [rounds[-1][:1], rounds[-1][1:]]
    for masks_now in rounds[:-1]:
        if len(masks_now) == 1:
            total = part.astype(jnp.float32) + exchange(part, axis, masks_now[0]).astype(jnp.float32)
        else:
            low, high = masks_now
            near = exchange(part, axis, low)
            far = exchange(part, axis, high)
            both = exchange(part, axis, low | high)
            total = (part.astype(jnp.float32) + near.astype(jnp.float32)) + (
                far.astype(jnp.float32) + both.astype(jnp.float32)
            )
        part = total.astype(jnp.bfloat16)
    return part, exchange(part, axis, rounds[-1][0])


def trade(own, other, slots_here, slots_there, axis):
    rows = jnp.arange(own.shape[axis])
    hits = slots_here[None, :] == rows[:, None]
    picks = jnp.any(
        hits[:, :, None] & (slots_there[None, :, None] == rows[None, None, :]), axis=1
    ).astype(own.dtype)
    moved = jnp.tensordot(picks, other, axes=((1,), (axis,)), preferred_element_type=jnp.float32)
    moved = jnp.moveaxis(moved, 0, axis).astype(own.dtype)
    shape = [1] * own.ndim
    shape[axis] = -1
    return jnp.where(jnp.any(hits, axis=1).reshape(shape), moved, own)


def per_device(
    hidden_in,
    norm_gain,
    w_query,
    w_key_value,
    w_output,
    cache_keys,
    cache_values,
    cache_lengths,
    remaining_steps,
    move_from,
    move_to,
):
    bf16, f32 = jnp.bfloat16, jnp.float32
    seq_count, width = hidden_in.shape
    model_size = lax.axis_size("mp")
    model_index = lax.axis_index("mp")
    group_index = lax.axis_index("dp")
    heads_here = w_query.shape[1] // HD
    kv_width = cache_keys.shape[2]
    kv_heads = kv_width // HD
    block_len = cache_keys.shape[1]
    col_width = w_key_value.shape[1]
    one_head_each = model_size == kv_heads and col_width == 2 * HD

    lengths = lax.dynamic_slice_in_dim(cache_lengths, group_index * seq_count, seq_count)
    remaining = lax.dynamic_slice_in_dim(remaining_steps, group_index * seq_count, seq_count)
    own_head = model_index * kv_heads // model_size
    flags = jnp.stack(
        [
            model_index,
            (model_index < model_size // 2).astype(jnp.int32),
            (model_index % 2 == 0).astype(jnp.int32) if one_head_each else jnp.int32(1),
            model_index * block_len if one_head_each else jnp.int32(0),
        ]
    )

    if one_head_each:
        half_size = model_size // 2
        across = list(range(half_size, model_size))
        masks = across[:2] + list(range(1, half_size)) + across[2:] + [0]
        shape = jax.ShapeDtypeStruct((2, seq_count, block_len, HD), bf16)
        packed = pl.pallas_call(
            functools.partial(pack_kernel, masks),
            out_shape=[shape] * model_size,
            in_specs=[in_smem, in_vmem, in_vmem],
            out_specs=[in_vmem] * model_size,
            compiler_params=pltpu.CompilerParams(vmem_limit_bytes=SMALL_VMEM),
        )(flags, cache_keys, cache_values)
        caches = [
            block if mask == 0 else exchange(block, "mp", mask)
            for mask, block in zip(masks, packed)
        ]
    else:
        masks = [0]
        both = jnp.stack([cache_keys, cache_values]).reshape(
            2, seq_count, block_len, kv_heads, HD
        )
        to_all = jnp.repeat(jnp.moveaxis(both, 3, 0), model_size // kv_heads, axis=0)
        caches = [lax.all_to_all(to_all, "mp", 0, 0, tiled=True)]

    half = HD // 2
    frequency = rope_base ** (-jnp.arange(half).astype(f32) * 2.0 / HD)
    positions = lengths[None, :] + jnp.arange(STEPS)[:, None]
    angles = positions.astype(f32)[:, :, None] * frequency[None, None, :]
    cosine, sine = jnp.cos(angles), jnp.sin(angles)
    tables = jnp.stack(
        [
            jnp.concatenate([cosine, cosine], axis=-1),
            jnp.concatenate([-sine, sine], axis=-1),
        ],
        axis=1,
    )
    remaining_rows = jnp.broadcast_to(remaining[:, None], (seq_count, HD))

    gain = norm_gain.reshape(1, width)
    hidden = hidden_in
    terms = ()
    fresh, kv_outputs = [], []
    row_f32 = jax.ShapeDtypeStruct((heads_here, seq_count, HD), f32)
    row_bf16 = jax.ShapeDtypeStruct((seq_count, width), bf16)
    head_row = jax.ShapeDtypeStruct((seq_count, HD), bf16)
    for step in range(STEPS):
        outs = [row_bf16, jax.ShapeDtypeStruct((seq_count, col_width), bf16)]
        outs = [row_bf16] * (step > 0) + outs + [head_row] * (2 * one_head_each)
        made = pl.pallas_call(
            functools.partial(norm_kernel, step, one_head_each),
            out_shape=outs,
            in_specs=[in_smem] + [in_vmem] * (5 + len(terms)),
            out_specs=[in_vmem] * len(outs),
            compiler_params=pltpu.CompilerParams(vmem_limit_bytes=SMALL_VMEM),
        )(flags, tables, remaining_rows, gain, w_key_value, hidden, *terms)
        if step > 0:
            hidden, *made = made
        normed, raw, *sent = made
        if one_head_each:
            kv_outputs.append(raw)
            pairs = model_size // 2
            to_even = [(low, 2 * low) for low in range(pairs)]
            to_odd = [(low, 2 * low + 1) for low in range(pairs)]
            fresh.append(
                lax.ppermute(sent[0], "mp", to_even + [(pairs + a, b) for a, b in to_odd])
            )
            fresh.append(
                lax.ppermute(sent[1], "mp", to_odd + [(pairs + a, b) for a, b in to_even])
            )
        else:
            raw_full = lax.all_gather(raw, "mp", axis=1, tiled=True)
            key_part = raw_full[:, :kv_width].astype(f32).reshape(seq_count, kv_heads, HD)
            key_part = root_norm(key_part)
            swapped = jnp.concatenate([key_part[..., half:], key_part[..., :half]], axis=-1)
            new_keys = (
                key_part * tables[step, 0][:, None, :] + swapped * tables[step, 1][:, None, :]
            ).astype(bf16)
            new_values = raw_full[:, kv_width:].reshape(seq_count, kv_heads, HD)
            live = (remaining > step)[:, None, None]
            new_kv = jnp.where(live, jnp.concatenate([new_keys, new_values], axis=1), 0)
            kv_outputs.append(
                lax.dynamic_slice_in_dim(
                    new_kv.reshape(seq_count, 2 * kv_width), model_index * col_width, col_width, 1
                )
            )
            fresh.append(lax.dynamic_index_in_dim(new_kv, own_head, 1, False))
            fresh.append(lax.dynamic_index_in_dim(new_kv, kv_heads + own_head, 1, False))
        attention = pl.pallas_call(
            functools.partial(query_kernel, step, masks),
            out_shape=[row_f32] * 4,
            in_specs=[in_smem] * 2 + [in_vmem] * (3 + len(caches)),
            out_specs=[in_vmem] * 4,
            cost_estimate=pl.CostEstimate(
                flops=2 * seq_count * width * heads_here * HD,
                bytes_accessed=2 * width * heads_here * HD,
                transcendentals=0,
            ),
            compiler_params=pltpu.CompilerParams(vmem_limit_bytes=KERNEL_VMEM),
        )(flags, lengths, tables, normed, w_query, *caches)
        part = pl.pallas_call(
            output_kernel,
            out_shape=row_bf16,
            in_specs=[in_smem] + [in_vmem] * (5 + len(fresh)),
            out_specs=in_vmem,
            compiler_params=pltpu.CompilerParams(vmem_limit_bytes=KERNEL_VMEM),
        )(flags, *attention, w_output, *fresh)
        terms = sum_rounds(part, "mp")
    update = terms[0].astype(f32) + terms[1].astype(f32)
    hidden_float = hidden.astype(f32)
    hidden = jnp.where(
        (remaining > STEPS - 1)[:, None], hidden_float + update, hidden_float
    ).astype(bf16)
    kv_local = jnp.stack(kv_outputs)

    slots_here = jnp.where(group_index == 0, move_from, move_to)
    slots_there = jnp.where(group_index == 0, move_to, move_from)
    other_kv = exchange(kv_local, "dp", 1)
    other_hidden = exchange(hidden, "dp", 1)
    return (
        trade(hidden, other_hidden, slots_here, slots_there, 0),
        trade(kv_local, other_kv, slots_here, slots_there, 1),
    )


def solution(mesh):
    placed = (
        P(("parts", "dp"), None),
        P(),
        P(None, "mp"),
        P(None, "mp"),
        P("mp", None),
        P(("parts", "dp"), "mp", None),
        P(("parts", "dp"), "mp", None),
        P("parts"),
        P("parts"),
        P("parts"),
        P("parts"),
    )
    return jax.shard_map(
        per_device,
        mesh=mesh,
        in_specs=placed,
        out_specs=(P(("parts", "dp"), None), P(None, ("parts", "dp"), "mp")),
        check_vma=False,
    )
```

```python
import functools
import math

import jax
import jax.numpy as jnp
from jax import lax
from jax.experimental import pallas as pl
from jax.experimental.pallas import tpu as pltpu
from jax.sharding import PartitionSpec as P

HD = 128
STEPS = 4
KERNEL_VMEM = 18 * 2**20


rope_base = 1000000.0
norm_eps = 1e-06

in_vmem = pl.BlockSpec(memory_space=pltpu.VMEM)
in_smem = pl.BlockSpec(memory_space=pltpu.SMEM)


def exchange(block, axis, mask):
    count = lax.axis_size(axis)
    return lax.ppermute(block, axis, [(low, low ^ mask) for low in range(count)])


def root_norm(values):
    return values * lax.rsqrt(jnp.mean(values * values, axis=-1, keepdims=True) + norm_eps)


def turn(values, cosine, sine):
    return values * cosine + pltpu.roll(values, values.shape[-1] // 2, 1) * sine


def prepare_kernel(block_len, one_head_each, flags_ref, lengths_ref, remaining_ref, from_ref, to_ref, tables_ref, tables_out, rows_out):
    me, group, count = flags_ref[0], flags_ref[1], flags_ref[2]
    seq_count = rows_out.shape[1]
    tables_out[...] = tables_ref[group]
    rows = lax.broadcasted_iota(jnp.int32, rows_out.shape[1:], 0)

    def fill(value):
        return jnp.full(rows.shape, value, jnp.int32)

    remaining, lengths = fill(0), fill(0)
    for seq in range(seq_count):
        remaining = jnp.where(rows == seq, remaining_ref[group * seq_count + seq], remaining)
        lengths = jnp.where(rows == seq, lengths_ref[group * seq_count + seq], lengths)
    rows_out[0] = remaining
    rows_out[1] = lengths
    rows_out[2] = fill((2 * me < count).astype(jnp.int32))
    rows_out[3] = fill(((me & 1) == 0).astype(jnp.int32) if one_head_each else 1)
    rows_out[4] = fill(me * block_len if one_head_each else 0)
    for move in range(from_ref.shape[0]):
        rows_out[5 + 2 * move] = fill(jnp.where(group == 0, from_ref[move], to_ref[move]))
        rows_out[6 + 2 * move] = fill(jnp.where(group == 0, to_ref[move], from_ref[move]))


def pack_kernel(masks, flags_ref, keys_ref, values_ref, *outs):
    me = flags_ref[0]
    for mask, out in zip(masks, outs):
        head = pl.multiple_of((me ^ mask) * HD, HD)
        out[0] = keys_ref[:, :, pl.ds(head, HD)]
        out[1] = values_ref[:, :, pl.ds(head, HD)]


def updated(step, rows_ref, hidden_ref, first_ref, second_ref):
    hidden = hidden_ref[...].astype(jnp.float32)
    update = first_ref[...].astype(jnp.float32) + second_ref[...].astype(jnp.float32)
    return jnp.where(rows_ref[0][:, :1] > step, hidden + update, hidden)


def add_kernel(*refs):
    terms = [ref[...].astype(jnp.float32) for ref in refs[:-1]]
    while len(terms) > 1:
        terms = [one + other for one, other in zip(terms[0::2], terms[1::2])]
    refs[-1][...] = terms[0].astype(jnp.bfloat16)


def norm_kernel(step, split_heads, rows_ref, tables_ref, gain_ref, w_ref, *refs):
    if step > 0:
        hidden_ref, first_ref, second_ref, hidden_out, *refs = refs
        hidden = updated(step - 1, rows_ref, hidden_ref, first_ref, second_ref).astype(jnp.bfloat16)
        hidden_out[...] = hidden
        hidden = hidden.astype(jnp.float32)
    else:
        hidden_ref, *refs = refs
        hidden = hidden_ref[...].astype(jnp.float32)
    normed = (root_norm(hidden) * gain_ref[...]).astype(jnp.bfloat16)
    normed_out, raw_out, *refs = refs
    normed_out[...] = normed
    raw = jnp.dot(normed, w_ref[...], preferred_element_type=jnp.float32).astype(jnp.bfloat16)
    if not split_heads:
        raw_out[...] = raw
        return
    is_key = rows_ref[2] > 0
    live = rows_ref[0] > step
    done = []
    for head in range(2):
        piece = raw[:, head * HD : (head + 1) * HD].astype(jnp.float32)
        turned = turn(root_norm(piece), tables_ref[step, 0], tables_ref[step, 1])
        done.append(jnp.where(live, jnp.where(is_key, turned, piece), 0.0))
        raw_out[:, head * HD : (head + 1) * HD] = done[head].astype(jnp.bfloat16)
    a_out, b_out = refs
    a_out[...] = jnp.where(is_key, done[0], done[1]).astype(jnp.bfloat16)
    b_out[...] = jnp.where(is_key, done[1], done[0]).astype(jnp.bfloat16)


def query_kernel(step, masks, rows_ref, tables_ref, normed_ref, w_ref, *rest):
    caches, rest = rest[: len(masks)], rest[len(masks) :]
    query_out, num_out, max_out, den_out = rest
    caches = [cache for _, cache in sorted(zip(masks, caches), key=lambda pair: pair[0])]
    seq_count = normed_ref.shape[0]
    heads = w_ref.shape[1] // HD
    projected = jnp.dot(normed_ref[...], w_ref[...], preferred_element_type=jnp.float32)
    for head in range(heads):
        piece = projected[:, head * HD : (head + 1) * HD]
        turned = turn(root_norm(piece), tables_ref[step, 0], tables_ref[step, 1])
        query_out[head] = turned.astype(jnp.bfloat16).astype(jnp.float32)

    def rows(which, seq):
        return jnp.concatenate(
            [
                ref[which, seq] if ref.ndim == 4 else ref[:, which, seq].reshape(-1, HD)
                for ref in caches
            ],
            axis=0,
        )

    scores = [
        lax.dot_general(
            query_out[:, seq, :].astype(jnp.bfloat16),
            rows(0, seq),
            (((1,), (1,)), ((), ())),
            preferred_element_type=jnp.float32,
        )
        * (1.0 / math.sqrt(HD))
        for seq in range(seq_count)
    ]
    places = lax.broadcasted_iota(jnp.int32, scores[0].shape, 1) ^ rows_ref[4][:1, :1]
    lengths = rows_ref[1]
    valids = [places < lengths[seq : seq + 1, :1] for seq in range(seq_count)]
    tops = [
        jnp.max(jnp.where(valid, score, -1e30), axis=-1, keepdims=True)
        for valid, score in zip(valids, scores)
    ]
    weights = [
        jnp.where(valid, jnp.exp(score - top), 0.0).astype(jnp.bfloat16)
        for valid, score, top in zip(valids, scores, tops)
    ]
    for seq in range(seq_count):
        num_out[:, seq, :] = jnp.dot(
            weights[seq], rows(1, seq), preferred_element_type=jnp.float32
        )
        mass = jnp.sum(weights[seq].astype(jnp.float32), axis=-1, keepdims=True)
        max_out[:, seq, :] = jnp.broadcast_to(tops[seq], (heads, HD))
        den_out[:, seq, :] = jnp.broadcast_to(mass, (heads, HD))


def output_kernel(rows_ref, query_ref, num_ref, max_ref, den_ref, w_ref, *rest):
    fresh, out_ref = rest[:-1], rest[-1]
    heads = query_ref.shape[0]
    key_first = rows_ref[3] > 0
    keys, values = [], []
    for one_ref, other_ref in zip(fresh[0::2], fresh[1::2]):
        one, other = one_ref[...].astype(jnp.float32), other_ref[...].astype(jnp.float32)
        keys.append(jnp.where(key_first, one, other))
        values.append(jnp.where(key_first, other, one))
    attended = []
    for head in range(heads):
        query = query_ref[head]
        scores = [
            jnp.sum(query * key, axis=-1, keepdims=True) * (1.0 / math.sqrt(HD)) for key in keys
        ]
        top_old = max_ref[head]
        top = functools.reduce(jnp.maximum, scores, top_old)
        scale = jnp.exp(top_old - top)
        num = scale * num_ref[head]
        den = scale * den_ref[head]
        for score, value in zip(scores, values):
            weight = jnp.exp(score - top).astype(jnp.bfloat16).astype(jnp.float32)
            num = num + weight * value
            den = den + weight
        attended.append((num / den).astype(jnp.bfloat16))
    out_ref[...] = jnp.dot(
        jnp.concatenate(attended, axis=1), w_ref[...], preferred_element_type=jnp.float32
    ).astype(jnp.bfloat16)


def final_kernel(step, rows_ref, hidden_ref, first_ref, second_ref, *refs):
    *raws, out_ref = refs
    width = hidden_ref.shape[1]
    out_ref[:, :width] = updated(step, rows_ref, hidden_ref, first_ref, second_ref).astype(
        jnp.bfloat16
    )
    for at, raw in enumerate(raws):
        columns = raw.shape[1]
        out_ref[:, width + at * columns : width + (at + 1) * columns] = raw[...]


def trade_kernel(moves, rows_ref, own_ref, other_ref, hidden_out, kv_out):
    rows = own_ref[...].astype(jnp.float32)
    other = other_ref[...].astype(jnp.float32)
    index = lax.broadcasted_iota(jnp.int32, rows.shape, 0)
    own = rows
    for move in range(moves):
        here, there = rows_ref[5 + 2 * move][:1, :1], rows_ref[6 + 2 * move][:1, :1]
        picked = jnp.sum(jnp.where(index == there, other, 0.0), axis=0, keepdims=True)
        own = jnp.where(index == here, picked, own)
    own = own.astype(jnp.bfloat16)
    width = hidden_out.shape[1]
    hidden_out[...] = own[:, :width]
    for step in range(kv_out.shape[0]):
        columns = kv_out.shape[2]
        kv_out[step] = own[:, width + step * columns : width + (step + 1) * columns]


def run(kernel, outs, *args, scalars=0, vmem=6 * 2**20, flops=0, moved=0):
    return pl.pallas_call(
        kernel,
        out_shape=outs,
        in_specs=[in_smem] * scalars + [in_vmem] * (len(args) - scalars),
        out_specs=jax.tree.map(lambda _: in_vmem, outs),
        cost_estimate=pl.CostEstimate(flops=flops, bytes_accessed=moved, transcendentals=0),
        compiler_params=pltpu.CompilerParams(vmem_limit_bytes=vmem),
    )(*args)


def sum_rounds(part, axis):
    masks = [1 << bit for bit in range(lax.axis_size(axis).bit_length() - 1)]
    *masks, last = masks
    while masks:
        now, masks = masks[:2], masks[2:]
        if len(now) == 2:
            now = now + [now[0] | now[1]]
        others = [exchange(part, axis, mask) for mask in now]
        part = run(add_kernel, jax.ShapeDtypeStruct(part.shape, part.dtype), part, *others)
    return part, exchange(part, axis, last)


def per_device(
    hidden_in,
    norm_gain,
    w_query,
    w_key_value,
    w_output,
    cache_keys,
    cache_values,
    cache_lengths,
    remaining_steps,
    move_from,
    move_to,
):
    bf16, f32 = jnp.bfloat16, jnp.float32
    seq_count, width = hidden_in.shape
    model_size = lax.axis_size("mp")
    model_index = lax.axis_index("mp")
    group_index = lax.axis_index("dp")
    heads_here = w_query.shape[1] // HD
    kv_width = cache_keys.shape[2]
    kv_heads = kv_width // HD
    block_len = cache_keys.shape[1]
    col_width = w_key_value.shape[1]
    one_head_each = model_size == kv_heads and col_width == 2 * HD

    def struct(*shape, dtype=bf16):
        return jax.ShapeDtypeStruct(shape, dtype)

    half = HD // 2
    frequency = rope_base ** (-jnp.arange(half).astype(f32) * 2.0 / HD)
    positions = cache_lengths.reshape(-1, 1, seq_count) + jnp.arange(STEPS)[None, :, None]
    angles = positions.astype(f32)[..., None] * frequency
    cosine, sine = jnp.cos(angles), jnp.sin(angles)
    tables = jnp.stack(
        [
            jnp.concatenate([cosine, cosine], axis=-1),
            jnp.concatenate([-sine, sine], axis=-1),
        ],
        axis=2,
    )
    flags = jnp.stack([model_index, group_index, jnp.int32(model_size)])
    moves = move_from.shape[0]
    own_head = model_index * kv_heads // model_size

    if one_head_each:
        half_size = model_size // 2
        across = list(range(half_size, model_size))
        within = list(range(1, half_size))
        masks = across[:2] + within + across[2:] + [0]
        packed = run(
            functools.partial(pack_kernel, masks),
            [struct(2, seq_count, block_len, HD)] * model_size,
            flags,
            cache_keys,
            cache_values,
            scalars=1,
        )
        blocks = dict(zip(masks, packed))
        landed = {0: blocks[0]}
        for mask in across[:2] + within:
            landed[mask] = exchange(blocks[mask], "mp", mask)
        for mask, earlier in zip(across[2:], within):
            sent, landed[earlier] = lax.optimization_barrier((blocks[mask], landed[earlier]))
            landed[mask] = exchange(sent, "mp", mask)
        caches = [landed[mask] for mask in masks]
    else:
        masks = [0]
        both = jnp.stack([cache_keys, cache_values]).reshape(
            2, seq_count, block_len, kv_heads, HD
        )
        to_all = jnp.repeat(jnp.moveaxis(both, 3, 0), model_size // kv_heads, axis=0)
        caches = [lax.all_to_all(to_all, "mp", 0, 0, tiled=True)]

    tables, rows = run(
        functools.partial(prepare_kernel, block_len, one_head_each),
        [struct(*tables.shape[1:], dtype=f32), struct(5 + 2 * moves, seq_count, HD, dtype=jnp.int32)],
        flags,
        cache_lengths,
        remaining_steps,
        move_from,
        move_to,
        tables,
        scalars=5,
    )
    gain = norm_gain.reshape(1, width)
    hidden = hidden_in
    terms = ()
    fresh, kv_outputs = [], []
    for step in range(STEPS):
        made = run(
            functools.partial(norm_kernel, step, one_head_each),
            [struct(seq_count, width)] * (1 + (step > 0))
            + [struct(seq_count, col_width)]
            + [struct(seq_count, HD)] * (2 * one_head_each),
            rows,
            tables,
            gain,
            w_key_value,
            hidden,
            *terms,
        )
        if step > 0:
            hidden, *made = made
        normed, raw, *sent = made
        if one_head_each:
            kv_outputs.append(raw)
            pairs = model_size // 2
            to_even = [(low, 2 * low) for low in range(pairs)]
            to_odd = [(low, 2 * low + 1) for low in range(pairs)]
            fresh.append(
                lax.ppermute(sent[0], "mp", to_even + [(pairs + a, b) for a, b in to_odd])
            )
            fresh.append(
                lax.ppermute(sent[1], "mp", to_odd + [(pairs + a, b) for a, b in to_even])
            )
        else:
            raw_full = lax.all_gather(raw, "mp", axis=1, tiled=True)
            key_part = raw_full[:, :kv_width].astype(f32).reshape(seq_count, kv_heads, HD)
            key_part = root_norm(key_part)
            swapped = jnp.concatenate([key_part[..., half:], key_part[..., :half]], axis=-1)
            new_keys = (
                key_part * tables[step, 0][:, None, :] + swapped * tables[step, 1][:, None, :]
            ).astype(bf16)
            new_values = raw_full[:, kv_width:].reshape(seq_count, kv_heads, HD)
            live = (rows[0] > step)[:, None, :]
            new_kv = jnp.where(live, jnp.concatenate([new_keys, new_values], axis=1), 0)
            kv_outputs.append(
                lax.dynamic_slice_in_dim(
                    new_kv.reshape(seq_count, 2 * kv_width), model_index * col_width, col_width, 1
                )
            )
            fresh.append(lax.dynamic_index_in_dim(new_kv, own_head, 1, False))
            fresh.append(lax.dynamic_index_in_dim(new_kv, kv_heads + own_head, 1, False))
        attention = run(
            functools.partial(query_kernel, step, masks),
            [struct(heads_here, seq_count, HD, dtype=f32)] * 4,
            rows,
            tables,
            normed,
            w_query,
            *caches,
            vmem=KERNEL_VMEM,
            flops=2 * seq_count * width * heads_here * HD,
            moved=2 * width * heads_here * HD,
        )
        part = run(
            output_kernel,
            struct(seq_count, width),
            rows,
            *attention,
            w_output,
            *fresh,
            vmem=KERNEL_VMEM,
        )
        terms = sum_rounds(part, "mp")

    own = run(
        functools.partial(final_kernel, STEPS - 1),
        struct(seq_count, width + STEPS * col_width),
        rows,
        hidden,
        *terms,
        *kv_outputs,
    )
    return tuple(
        run(
            functools.partial(trade_kernel, moves),
            [struct(seq_count, width), struct(STEPS, seq_count, col_width)],
            rows,
            own,
            exchange(own, "dp", 1),
        )
    )


def solution(mesh):
    placed = (
        P(("parts", "dp"), None),
        P(),
        P(None, "mp"),
        P(None, "mp"),
        P("mp", None),
        P(("parts", "dp"), "mp", None),
        P(("parts", "dp"), "mp", None),
        P("parts"),
        P("parts"),
        P("parts"),
        P("parts"),
    )
    return jax.shard_map(
        per_device,
        mesh=mesh,
        in_specs=placed,
        out_specs=(P(("parts", "dp"), None), P(None, ("parts", "dp"), "mp")),
        check_vma=False,
    )
```

```python
import functools
import math

import jax
import jax.numpy as jnp
from jax import lax
from jax.experimental import pallas as pl
from jax.experimental.pallas import tpu as pltpu
from jax.sharding import PartitionSpec as P

HD = 128
STEPS = 4
KERNEL_VMEM = 18 * 2**20
LOAD_VMEM = 28 * 2**20
COPY_VMEM = 8 * 2**20


rope_base = 1000000.0
norm_eps = 1e-06

in_vmem = pl.BlockSpec(memory_space=pltpu.VMEM)
in_smem = pl.BlockSpec(memory_space=pltpu.SMEM)
in_place = pl.BlockSpec(memory_space=pltpu.HBM)


def exchange(block, axis, mask):
    count = lax.axis_size(axis)
    return lax.ppermute(block, axis, [(low, low ^ mask) for low in range(count)])


def root_norm(values):
    return values * lax.rsqrt(jnp.mean(values * values, axis=-1, keepdims=True) + norm_eps)


def turn(values, cosine, sine):
    return values * cosine + pltpu.roll(values, values.shape[-1] // 2, 1) * sine


def prepare_kernel(block_len, one_head_each, total, moves, scalars_ref, tables_ref, tables_out, rows_out):
    me, group, count = scalars_ref[0], scalars_ref[1], scalars_ref[2]
    seq_count = rows_out.shape[1]
    first = pl.multiple_of(group * seq_count, seq_count)
    tables_out[...] = tables_ref[:, :, pl.ds(first, seq_count), :]
    rows = lax.broadcasted_iota(jnp.int32, rows_out.shape[1:], 0)

    def fill(value):
        return jnp.full(rows.shape, value, jnp.int32)

    remaining, lengths = fill(0), fill(0)
    for seq in range(seq_count):
        lengths = jnp.where(rows == seq, scalars_ref[3 + first + seq], lengths)
        remaining = jnp.where(rows == seq, scalars_ref[3 + total + first + seq], remaining)
    rows_out[0] = remaining
    rows_out[1] = lengths
    rows_out[2] = fill((2 * me < count).astype(jnp.int32))
    rows_out[3] = fill(((me & 1) == 0).astype(jnp.int32) if one_head_each else 1)
    rows_out[4] = fill(me * block_len if one_head_each else 0)
    for move in range(moves):
        slots = [scalars_ref[3 + 2 * total + moves * side + move] for side in range(2)]
        rows_out[5 + 2 * move] = fill(jnp.where(group == 0, slots[0], slots[1]))
        rows_out[6 + 2 * move] = fill(jnp.where(group == 0, slots[1], slots[0]))


def load_kernel(*refs):
    *refs, sems = refs
    count = len(refs) // 2
    copies = [
        pltpu.make_async_copy(source, target, sems.at[at])
        for at, (source, target) in enumerate(zip(refs[:count], refs[count:]))
    ]
    for copy in copies:
        copy.start()
    for copy in copies:
        copy.wait()


def updated(step, rows_ref, hidden_ref, first_ref, second_ref):
    hidden = hidden_ref[...].astype(jnp.float32)
    update = first_ref[...].astype(jnp.float32) + second_ref[...].astype(jnp.float32)
    return jnp.where(rows_ref[0][:, :1] > step, hidden + update, hidden)


def add_kernel(*refs):
    terms = [ref[...].astype(jnp.float32) for ref in refs[:-1]]
    while len(terms) > 1:
        terms = [one + other for one, other in zip(terms[0::2], terms[1::2])]
    refs[-1][...] = terms[0].astype(jnp.bfloat16)


def norm_kernel(step, split_heads, rows_ref, tables_ref, gain_ref, w_ref, *refs):
    if step > 0:
        hidden_ref, first_ref, second_ref, hidden_out, *refs = refs
        hidden = updated(step - 1, rows_ref, hidden_ref, first_ref, second_ref).astype(jnp.bfloat16)
        hidden_out[...] = hidden
        hidden = hidden.astype(jnp.float32)
    else:
        hidden_ref, *refs = refs
        hidden = hidden_ref[...].astype(jnp.float32)
    normed = (root_norm(hidden) * gain_ref[...]).astype(jnp.bfloat16)
    normed_out, raw_out, *refs = refs
    normed_out[...] = normed
    raw = jnp.dot(normed, w_ref[...], preferred_element_type=jnp.float32).astype(jnp.bfloat16)
    if not split_heads:
        raw_out[...] = raw
        return
    is_key = rows_ref[2] > 0
    live = rows_ref[0] > step
    done = []
    for head in range(2):
        piece = raw[:, head * HD : (head + 1) * HD].astype(jnp.float32)
        turned = turn(root_norm(piece), tables_ref[step, 0], tables_ref[step, 1])
        done.append(jnp.where(live, jnp.where(is_key, turned, piece), 0.0))
        raw_out[:, head * HD : (head + 1) * HD] = done[head].astype(jnp.bfloat16)
    a_out, b_out = refs
    a_out[...] = jnp.where(is_key, done[0], done[1]).astype(jnp.bfloat16)
    b_out[...] = jnp.where(is_key, done[1], done[0]).astype(jnp.bfloat16)


def project_kernel(step, tables_ref, normed_ref, w_ref, query_out):
    projected = jnp.dot(normed_ref[...], w_ref[...], preferred_element_type=jnp.float32)
    for head in range(query_out.shape[0]):
        piece = projected[:, head * HD : (head + 1) * HD]
        turned = turn(root_norm(piece), tables_ref[step, 0], tables_ref[step, 1])
        query_out[head] = turned.astype(jnp.bfloat16).astype(jnp.float32)


def query_kernel(step, masks, rows_ref, tables_ref, normed_ref, w_ref, *rest):
    *caches, query_out, num_out, max_out, den_out = rest
    project_kernel(step, tables_ref, normed_ref, w_ref, query_out)
    attend_kernel(masks, rows_ref, query_out, *caches, num_out, max_out, den_out)


def attend_kernel(masks, rows_ref, query_ref, *rest):
    *caches, num_out, max_out, den_out = rest
    caches = [cache for _, cache in sorted(zip(masks, caches), key=lambda pair: pair[0])]
    heads, seq_count = query_ref.shape[:2]

    def rows(which, seq):
        return jnp.concatenate(
            [
                ref[which, seq] if ref.ndim == 4 else ref[:, which, seq].reshape(-1, HD)
                for ref in caches
            ],
            axis=0,
        )

    scores = [
        lax.dot_general(
            query_ref[:, seq, :].astype(jnp.bfloat16),
            rows(0, seq),
            (((1,), (1,)), ((), ())),
            preferred_element_type=jnp.float32,
        )
        * (1.0 / math.sqrt(HD))
        for seq in range(seq_count)
    ]
    places = lax.broadcasted_iota(jnp.int32, scores[0].shape, 1) ^ rows_ref[4][:1, :1]
    lengths = rows_ref[1]
    valids = [places < lengths[seq : seq + 1, :1] for seq in range(seq_count)]
    tops = [
        jnp.max(jnp.where(valid, score, -1e30), axis=-1, keepdims=True)
        for valid, score in zip(valids, scores)
    ]
    weights = [
        jnp.where(valid, jnp.exp(score - top), 0.0).astype(jnp.bfloat16)
        for valid, score, top in zip(valids, scores, tops)
    ]
    for seq in range(seq_count):
        num_out[:, seq, :] = jnp.dot(
            weights[seq], rows(1, seq), preferred_element_type=jnp.float32
        )
        mass = jnp.sum(weights[seq].astype(jnp.float32), axis=-1, keepdims=True)
        max_out[:, seq, :] = jnp.broadcast_to(tops[seq], (heads, HD))
        den_out[:, seq, :] = jnp.broadcast_to(mass, (heads, HD))


def output_kernel(rows_ref, query_ref, num_ref, max_ref, den_ref, w_ref, *rest):
    fresh, out_ref = rest[:-1], rest[-1]
    heads = query_ref.shape[0]
    key_first = rows_ref[3] > 0
    keys, values = [], []
    for one_ref, other_ref in zip(fresh[0::2], fresh[1::2]):
        one, other = one_ref[...].astype(jnp.float32), other_ref[...].astype(jnp.float32)
        keys.append(jnp.where(key_first, one, other))
        values.append(jnp.where(key_first, other, one))
    attended = []
    for head in range(heads):
        query = query_ref[head]
        scores = [
            jnp.sum(query * key, axis=-1, keepdims=True) * (1.0 / math.sqrt(HD)) for key in keys
        ]
        top_old = max_ref[head]
        top = functools.reduce(jnp.maximum, scores, top_old)
        scale = jnp.exp(top_old - top)
        num = scale * num_ref[head]
        den = scale * den_ref[head]
        for score, value in zip(scores, values):
            weight = jnp.exp(score - top).astype(jnp.bfloat16).astype(jnp.float32)
            num = num + weight * value
            den = den + weight
        attended.append((num / den).astype(jnp.bfloat16))
    out_ref[...] = jnp.dot(
        jnp.concatenate(attended, axis=1), w_ref[...], preferred_element_type=jnp.float32
    ).astype(jnp.bfloat16)


def final_kernel(step, rows_ref, hidden_ref, first_ref, second_ref, *refs):
    *raws, out_ref, sent_ref = refs
    last = updated(step, rows_ref, hidden_ref, first_ref, second_ref).astype(jnp.bfloat16)
    own = jnp.concatenate([last] + [raw[...] for raw in raws], axis=1)
    out_ref[...] = own
    own = own.astype(jnp.float32)
    index = lax.broadcasted_iota(jnp.int32, own.shape, 0)
    moved = [
        jnp.sum(jnp.where(index == rows_ref[5 + 2 * move][:1, :1], own, 0.0), axis=0, keepdims=True)
        for move in range(sent_ref.shape[0])
    ]
    sent_ref[...] = jnp.concatenate(moved, axis=0).astype(jnp.bfloat16)


def trade_kernel(rows_ref, own_ref, got_ref, hidden_out, kv_out):
    own = own_ref[...].astype(jnp.float32)
    got = got_ref[...].astype(jnp.float32)
    index = lax.broadcasted_iota(jnp.int32, own.shape, 0)
    for move in range(got.shape[0]):
        own = jnp.where(index == rows_ref[5 + 2 * move][:1, :1], got[move : move + 1], own)
    own = own.astype(jnp.bfloat16)
    width = hidden_out.shape[1]
    hidden_out[...] = own[:, :width]
    for step in range(kv_out.shape[0]):
        columns = kv_out.shape[2]
        kv_out[step] = own[:, width + step * columns : width + (step + 1) * columns]


def after(one, *others):
    return lax.optimization_barrier((one, *others))[0] if others else one


def run(kernel, outs, *args, scalars=0, copies=0, vmem=6 * 2**20, flops=0, moved=0):
    return pl.pallas_call(
        kernel,
        out_shape=outs,
        in_specs=[in_smem] * scalars + [in_place if copies else in_vmem] * (len(args) - scalars),
        out_specs=jax.tree.map(lambda _: in_vmem, outs),
        scratch_shapes=[pltpu.SemaphoreType.DMA((copies,))] if copies else [],
        cost_estimate=pl.CostEstimate(flops=flops, bytes_accessed=moved, transcendentals=0),
        compiler_params=pltpu.CompilerParams(vmem_limit_bytes=vmem),
    )(*args)


def sum_rounds(part, axis):
    masks = [1 << bit for bit in range(lax.axis_size(axis).bit_length() - 1)]
    *masks, last = masks
    while masks:
        now, masks = masks[:2], masks[2:]
        if len(now) == 2:
            now = now + [now[0] | now[1]]
        others = [exchange(part, axis, mask) for mask in now]
        part = run(add_kernel, jax.ShapeDtypeStruct(part.shape, part.dtype), part, *others)
    return part, exchange(part, axis, last)


def per_device(
    hidden_in,
    norm_gain,
    w_query,
    w_key_value,
    w_output,
    cache_keys,
    cache_values,
    cache_lengths,
    remaining_steps,
    move_from,
    move_to,
):
    bf16, f32 = jnp.bfloat16, jnp.float32
    seq_count, width = hidden_in.shape
    model_size = lax.axis_size("mp")
    model_index = lax.axis_index("mp")
    group_index = lax.axis_index("dp")
    heads_here = w_query.shape[1] // HD
    kv_width = cache_keys.shape[2]
    kv_heads = kv_width // HD
    block_len = cache_keys.shape[1]
    col_width = w_key_value.shape[1]
    one_head_each = model_size == kv_heads and col_width == 2 * HD

    def struct(*shape, dtype=bf16):
        return jax.ShapeDtypeStruct(shape, dtype)

    half = HD // 2
    frequency = rope_base ** (-(jnp.arange(HD) % half).astype(f32) * 2.0 / HD)
    positions = cache_lengths[None, :] + jnp.arange(STEPS)[:, None]
    angles = positions.astype(f32)[..., None] * frequency
    sign = jnp.where(jnp.arange(HD) < half, -1.0, 1.0)
    tables = jnp.stack([jnp.cos(angles), jnp.sin(angles) * sign], axis=1)
    total, moves = cache_lengths.shape[0], move_from.shape[0]
    place = jnp.stack([model_index, group_index, jnp.int32(model_size)])
    scalars = jnp.concatenate([place, cache_lengths, remaining_steps, move_from, move_to])
    own_head = model_index * kv_heads // model_size

    if one_head_each:
        half_size = model_size // 2
        across = list(range(half_size, model_size))
        within = list(range(1, half_size))
        masks = across[:2] + within + across[2:] + [0]
        landed = {}
        for mask in masks:
            head = (model_index ^ mask) * HD
            block = jnp.stack(
                [
                    lax.dynamic_slice_in_dim(cache, head, HD, 2)
                    for cache in (cache_keys, cache_values)
                ]
            )
            if mask in across[2:]:
                block = after(block, landed[within[mask - across[2]]])
            landed[mask] = exchange(block, "mp", mask) if mask else block
        caches = [landed[mask] for mask in masks]
    else:
        masks = [0]
        both = jnp.stack([cache_keys, cache_values]).reshape(
            2, seq_count, block_len, kv_heads, HD
        )
        to_all = jnp.repeat(jnp.moveaxis(both, 3, 0), model_size // kv_heads, axis=0)
        caches = [lax.all_to_all(to_all, "mp", 0, 0, tiled=True)]

    tables, rows = run(
        functools.partial(prepare_kernel, block_len, one_head_each, total, moves),
        [
            struct(STEPS, 2, seq_count, HD, dtype=f32),
            struct(5 + 2 * moves, seq_count, HD, dtype=jnp.int32),
        ],
        scalars,
        tables,
        scalars=1,
    )

    def load(*arrays, vmem):
        return run(
            load_kernel,
            [struct(*array.shape, dtype=array.dtype) for array in arrays],
            *arrays,
            copies=len(arrays),
            vmem=vmem,
            moved=sum(array.size * array.dtype.itemsize for array in arrays),
        )

    gain = norm_gain.reshape(1, width)
    w_key_value, hidden, gain = load(w_key_value, hidden_in, gain, vmem=COPY_VMEM)
    terms = ()
    fresh, kv_outputs = [], []
    for step in range(STEPS):
        made = run(
            functools.partial(norm_kernel, step, one_head_each),
            [struct(seq_count, width)] * (1 + (step > 0))
            + [struct(seq_count, col_width)]
            + [struct(seq_count, HD)] * (2 * one_head_each),
            rows,
            tables,
            gain,
            w_key_value,
            hidden,
            *terms,
        )
        if step > 0:
            hidden, *made = made
        normed, raw, *sent = made
        if one_head_each:
            kv_outputs.append(raw)
            pairs = model_size // 2
            to_even = [(low, 2 * low) for low in range(pairs)]
            to_odd = [(low, 2 * low + 1) for low in range(pairs)]
            fresh.append(
                lax.ppermute(sent[0], "mp", to_even + [(pairs + a, b) for a, b in to_odd])
            )
            fresh.append(
                lax.ppermute(sent[1], "mp", to_odd + [(pairs + a, b) for a, b in to_even])
            )
        else:
            raw_full = lax.all_gather(raw, "mp", axis=1, tiled=True)
            key_part = raw_full[:, :kv_width].astype(f32).reshape(seq_count, kv_heads, HD)
            key_part = root_norm(key_part)
            swapped = jnp.concatenate([key_part[..., half:], key_part[..., :half]], axis=-1)
            new_keys = (
                key_part * tables[step, 0][:, None, :] + swapped * tables[step, 1][:, None, :]
            ).astype(bf16)
            new_values = raw_full[:, kv_width:].reshape(seq_count, kv_heads, HD)
            live = (rows[0] > step)[:, None, :]
            new_kv = jnp.where(live, jnp.concatenate([new_keys, new_values], axis=1), 0)
            kv_outputs.append(
                lax.dynamic_slice_in_dim(
                    new_kv.reshape(seq_count, 2 * kv_width), model_index * col_width, col_width, 1
                )
            )
            fresh.append(lax.dynamic_index_in_dim(new_kv, own_head, 1, False))
            fresh.append(lax.dynamic_index_in_dim(new_kv, kv_heads + own_head, 1, False))
        if step == 0:
            w_query, w_output = load(w_query, w_output, vmem=LOAD_VMEM)
        sums = [struct(heads_here, seq_count, HD, dtype=f32)] * 4
        cost = {"flops": 2 * seq_count * width * heads_here * HD, "moved": 2 * width * heads_here * HD}
        if step > 0:
            attention = run(
                functools.partial(query_kernel, step, masks),
                sums,
                rows,
                tables,
                normed,
                w_query,
                *caches,
                vmem=KERNEL_VMEM,
                **cost,
            )
        else:
            queries = run(
                functools.partial(project_kernel, step),
                sums[0],
                tables,
                normed,
                w_query,
                vmem=KERNEL_VMEM,
                **cost,
            )
            attention = run(functools.partial(attend_kernel, masks), sums[1:], rows, queries, *caches)
            attention = [queries, *attention]
        part = run(
            output_kernel,
            struct(seq_count, width),
            rows,
            *attention,
            w_output,
            *fresh,
            vmem=KERNEL_VMEM,
        )
        terms = sum_rounds(part, "mp")

    own, sent = run(
        functools.partial(final_kernel, STEPS - 1),
        [struct(seq_count, width + STEPS * col_width), struct(moves, width + STEPS * col_width)],
        rows,
        hidden,
        *terms,
        *kv_outputs,
    )
    return tuple(
        run(
            trade_kernel,
            [struct(seq_count, width), struct(STEPS, seq_count, col_width)],
            rows,
            own,
            exchange(sent, "dp", 1),
        )
    )


def solution(mesh):
    placed = (
        P(("parts", "dp"), None),
        P(),
        P(None, "mp"),
        P(None, "mp"),
        P("mp", None),
        P(("parts", "dp"), "mp", None),
        P(("parts", "dp"), "mp", None),
        P("parts"),
        P("parts"),
        P("parts"),
        P("parts"),
    )
    return jax.shard_map(
        per_device,
        mesh=mesh,
        in_specs=placed,
        out_specs=(P(("parts", "dp"), None), P(None, ("parts", "dp"), "mp")),
        check_vma=False,
    )
```

```python
import functools
import math

import jax
import jax.numpy as jnp
from jax import lax
from jax.experimental import pallas as pl
from jax.experimental.pallas import tpu as pltpu
from jax.sharding import PartitionSpec as P

HD = 128
STEPS = 4
KERNEL_VMEM = 18 * 2**20
LOAD_VMEM = 28 * 2**20
COPY_VMEM = 8 * 2**20


rope_base = 1000000.0
norm_eps = 1e-06

in_vmem = pl.BlockSpec(memory_space=pltpu.VMEM)
in_smem = pl.BlockSpec(memory_space=pltpu.SMEM)
in_place = pl.BlockSpec(memory_space=pltpu.HBM)


def exchange(block, axis, mask):
    count = lax.axis_size(axis)
    return lax.ppermute(block, axis, [(low, low ^ mask) for low in range(count)])


def root_norm(values):
    return values * lax.rsqrt(jnp.mean(values * values, axis=-1, keepdims=True) + norm_eps)


def turn(values, cosine, sine):
    return values * cosine + pltpu.roll(values, values.shape[-1] // 2, 1) * sine


def prepare_kernel(block_len, one_head_each, total, moves, scalars_ref, tables_ref, tables_out, rows_out):
    me, group, count = scalars_ref[0], scalars_ref[1], scalars_ref[2]
    seq_count = rows_out.shape[1]
    first = pl.multiple_of(group * seq_count, seq_count)
    tables_out[...] = tables_ref[:, :, pl.ds(first, seq_count), :]
    rows = lax.broadcasted_iota(jnp.int32, rows_out.shape[1:], 0)

    def fill(value):
        return jnp.full(rows.shape, value, jnp.int32)

    remaining, lengths = fill(0), fill(0)
    for seq in range(seq_count):
        lengths = jnp.where(rows == seq, scalars_ref[3 + first + seq], lengths)
        remaining = jnp.where(rows == seq, scalars_ref[3 + total + first + seq], remaining)
    rows_out[0] = remaining
    rows_out[1] = lengths
    rows_out[2] = fill((2 * me < count).astype(jnp.int32))
    rows_out[3] = fill(((me & 1) == 0).astype(jnp.int32) if one_head_each else 1)
    rows_out[4] = fill(me * block_len if one_head_each else 0)
    for move in range(moves):
        slots = [scalars_ref[3 + 2 * total + moves * side + move] for side in range(2)]
        rows_out[5 + 2 * move] = fill(jnp.where(group == 0, slots[0], slots[1]))
        rows_out[6 + 2 * move] = fill(jnp.where(group == 0, slots[1], slots[0]))


def load_kernel(*refs):
    *refs, sems = refs
    count = len(refs) // 2
    copies = [
        pltpu.make_async_copy(source, target, sems.at[at])
        for at, (source, target) in enumerate(zip(refs[:count], refs[count:]))
    ]
    for copy in copies:
        copy.start()
    for copy in copies:
        copy.wait()


def updated(step, rows_ref, hidden_ref, first_ref, second_ref):
    hidden = hidden_ref[...].astype(jnp.float32)
    update = first_ref[...].astype(jnp.float32) + second_ref[...].astype(jnp.float32)
    return jnp.where(rows_ref[0][:, :1] > step, hidden + update, hidden)


def add_kernel(*refs):
    terms = [ref[...].astype(jnp.float32) for ref in refs[:-1]]
    while len(terms) > 1:
        terms = [one + other for one, other in zip(terms[0::2], terms[1::2])]
    refs[-1][...] = terms[0].astype(jnp.bfloat16)


def norm_kernel(step, split_heads, rows_ref, tables_ref, gain_ref, w_ref, *refs):
    if step > 0:
        hidden_ref, first_ref, second_ref, hidden_out, *refs = refs
        hidden = updated(step - 1, rows_ref, hidden_ref, first_ref, second_ref).astype(jnp.bfloat16)
        hidden_out[...] = hidden
        hidden = hidden.astype(jnp.float32)
    else:
        hidden_ref, *refs = refs
        hidden = hidden_ref[...].astype(jnp.float32)
    normed = (root_norm(hidden) * gain_ref[...]).astype(jnp.bfloat16)
    normed_out, raw_out, *refs = refs
    normed_out[...] = normed
    raw = jnp.dot(normed, w_ref[...], preferred_element_type=jnp.float32).astype(jnp.bfloat16)
    if not split_heads:
        raw_out[...] = raw
        return
    is_key = rows_ref[2] > 0
    live = rows_ref[0] > step
    done = []
    for head in range(2):
        piece = raw[:, head * HD : (head + 1) * HD].astype(jnp.float32)
        turned = turn(root_norm(piece), tables_ref[step, 0], tables_ref[step, 1])
        done.append(jnp.where(live, jnp.where(is_key, turned, piece), 0.0))
        raw_out[:, head * HD : (head + 1) * HD] = done[head].astype(jnp.bfloat16)
    a_out, b_out = refs
    a_out[...] = jnp.where(is_key, done[0], done[1]).astype(jnp.bfloat16)
    b_out[...] = jnp.where(is_key, done[1], done[0]).astype(jnp.bfloat16)


def project_kernel(step, tables_ref, normed_ref, w_ref, query_out):
    projected = jnp.dot(normed_ref[...], w_ref[...], preferred_element_type=jnp.float32)
    for head in range(query_out.shape[0]):
        piece = projected[:, head * HD : (head + 1) * HD]
        turned = turn(root_norm(piece), tables_ref[step, 0], tables_ref[step, 1])
        query_out[head] = turned.astype(jnp.bfloat16).astype(jnp.float32)


def query_kernel(step, masks, rows_ref, tables_ref, normed_ref, w_ref, *rest):
    *caches, query_out, num_out, max_out, den_out = rest
    project_kernel(step, tables_ref, normed_ref, w_ref, query_out)
    attend_kernel(masks, rows_ref, query_out, *caches, num_out, max_out, den_out)


def attend_kernel(masks, rows_ref, query_ref, *rest):
    *caches, num_out, max_out, den_out = rest
    caches = [cache for _, cache in sorted(zip(masks, caches), key=lambda pair: pair[0])]
    heads, seq_count = query_ref.shape[:2]

    def rows(which, seq):
        return jnp.concatenate(
            [
                ref[which, seq] if ref.ndim == 4 else ref[:, which, seq].reshape(-1, HD)
                for ref in caches
            ],
            axis=0,
        )

    scores = [
        lax.dot_general(
            query_ref[:, seq, :].astype(jnp.bfloat16),
            rows(0, seq),
            (((1,), (1,)), ((), ())),
            preferred_element_type=jnp.float32,
        )
        * (1.0 / math.sqrt(HD))
        for seq in range(seq_count)
    ]
    places = lax.broadcasted_iota(jnp.int32, scores[0].shape, 1) ^ rows_ref[4][:1, :1]
    lengths = rows_ref[1]
    valids = [places < lengths[seq : seq + 1, :1] for seq in range(seq_count)]
    tops = [
        jnp.max(jnp.where(valid, score, -1e30), axis=-1, keepdims=True)
        for valid, score in zip(valids, scores)
    ]
    weights = [
        jnp.where(valid, jnp.exp(score - top), 0.0).astype(jnp.bfloat16)
        for valid, score, top in zip(valids, scores, tops)
    ]
    for seq in range(seq_count):
        num_out[:, seq, :] = jnp.dot(
            weights[seq], rows(1, seq), preferred_element_type=jnp.float32
        )
        mass = jnp.sum(weights[seq].astype(jnp.float32), axis=-1, keepdims=True)
        max_out[:, seq, :] = jnp.broadcast_to(tops[seq], (heads, HD))
        den_out[:, seq, :] = jnp.broadcast_to(mass, (heads, HD))


def output_kernel(rows_ref, query_ref, num_ref, max_ref, den_ref, w_ref, *rest):
    fresh, out_ref = rest[:-1], rest[-1]
    heads = query_ref.shape[0]
    key_first = rows_ref[3] > 0
    keys, values = [], []
    for one_ref, other_ref in zip(fresh[0::2], fresh[1::2]):
        one, other = one_ref[...].astype(jnp.float32), other_ref[...].astype(jnp.float32)
        keys.append(jnp.where(key_first, one, other))
        values.append(jnp.where(key_first, other, one))
    attended = []
    for head in range(heads):
        query = query_ref[head]
        scores = [
            jnp.sum(query * key, axis=-1, keepdims=True) * (1.0 / math.sqrt(HD)) for key in keys
        ]
        top_old = max_ref[head]
        top = functools.reduce(jnp.maximum, scores, top_old)
        scale = jnp.exp(top_old - top)
        num = scale * num_ref[head]
        den = scale * den_ref[head]
        for score, value in zip(scores, values):
            weight = jnp.exp(score - top).astype(jnp.bfloat16).astype(jnp.float32)
            num = num + weight * value
            den = den + weight
        attended.append((num / den).astype(jnp.bfloat16))
    out_ref[...] = jnp.dot(
        jnp.concatenate(attended, axis=1), w_ref[...], preferred_element_type=jnp.float32
    ).astype(jnp.bfloat16)


def final_kernel(step, rows_ref, hidden_ref, first_ref, second_ref, *refs):
    *raws, out_ref, sent_ref = refs
    last = updated(step, rows_ref, hidden_ref, first_ref, second_ref).astype(jnp.bfloat16)
    own = jnp.concatenate([last] + [raw[...] for raw in raws], axis=1)
    out_ref[...] = own
    own = own.astype(jnp.float32)
    index = lax.broadcasted_iota(jnp.int32, own.shape, 0)
    moved = [
        jnp.sum(jnp.where(index == rows_ref[5 + 2 * move][:1, :1], own, 0.0), axis=0, keepdims=True)
        for move in range(sent_ref.shape[0])
    ]
    sent_ref[...] = jnp.concatenate(moved, axis=0).astype(jnp.bfloat16)


def trade_kernel(rows_ref, own_ref, got_ref, hidden_out, kv_out):
    own = own_ref[...].astype(jnp.float32)
    got = got_ref[...].astype(jnp.float32)
    index = lax.broadcasted_iota(jnp.int32, own.shape, 0)
    for move in range(got.shape[0]):
        own = jnp.where(index == rows_ref[5 + 2 * move][:1, :1], got[move : move + 1], own)
    own = own.astype(jnp.bfloat16)
    width = hidden_out.shape[1]
    hidden_out[...] = own[:, :width]
    for step in range(kv_out.shape[0]):
        columns = kv_out.shape[2]
        kv_out[step] = own[:, width + step * columns : width + (step + 1) * columns]


def run(kernel, outs, *args, scalars=0, copies=0, vmem=6 * 2**20, flops=0, moved=0):
    return pl.pallas_call(
        kernel,
        out_shape=outs,
        in_specs=[in_smem] * scalars + [in_place if copies else in_vmem] * (len(args) - scalars),
        out_specs=jax.tree.map(lambda _: in_vmem, outs),
        scratch_shapes=[pltpu.SemaphoreType.DMA((copies,))] if copies else [],
        cost_estimate=pl.CostEstimate(flops=flops, bytes_accessed=moved, transcendentals=0),
        compiler_params=pltpu.CompilerParams(vmem_limit_bytes=vmem),
    )(*args)


def sum_rounds(part, axis):
    masks = [1 << bit for bit in range(lax.axis_size(axis).bit_length() - 1)]
    *masks, last = masks
    while masks:
        now, masks = masks[:2], masks[2:]
        if len(now) == 2:
            now = now + [now[0] | now[1]]
        others = [exchange(part, axis, mask) for mask in now]
        part = run(add_kernel, jax.ShapeDtypeStruct(part.shape, part.dtype), part, *others)
    return part, exchange(part, axis, last)


def per_device(
    hidden_in,
    norm_gain,
    w_query,
    w_key_value,
    w_output,
    cache_keys,
    cache_values,
    cache_lengths,
    remaining_steps,
    move_from,
    move_to,
):
    bf16, f32 = jnp.bfloat16, jnp.float32
    seq_count, width = hidden_in.shape
    model_size = lax.axis_size("mp")
    model_index = lax.axis_index("mp")
    group_index = lax.axis_index("dp")
    heads_here = w_query.shape[1] // HD
    kv_width = cache_keys.shape[2]
    kv_heads = kv_width // HD
    block_len = cache_keys.shape[1]
    col_width = w_key_value.shape[1]
    one_head_each = model_size == kv_heads and col_width == 2 * HD

    def struct(*shape, dtype=bf16):
        return jax.ShapeDtypeStruct(shape, dtype)

    half = HD // 2
    frequency = rope_base ** (-(jnp.arange(HD) % half).astype(f32) * 2.0 / HD)
    positions = cache_lengths[None, :] + jnp.arange(STEPS)[:, None]
    angles = positions.astype(f32)[..., None] * frequency
    sign = jnp.where(jnp.arange(HD) < half, -1.0, 1.0)
    tables = jnp.stack([jnp.cos(angles), jnp.sin(angles) * sign], axis=1)
    total, moves = cache_lengths.shape[0], move_from.shape[0]
    place = jnp.stack([model_index, group_index, jnp.int32(model_size)])
    scalars = jnp.concatenate([place, cache_lengths, remaining_steps, move_from, move_to])
    own_head = model_index * kv_heads // model_size

    if one_head_each:
        half_size = model_size // 2
        across = list(range(half_size, model_size))
        within = list(range(1, half_size))
        masks = within + across + [0]
        landed = {}
        for mask in masks:
            head = (model_index ^ mask) * HD
            block = jnp.stack(
                [
                    lax.dynamic_slice_in_dim(cache, head, HD, 2)
                    for cache in (cache_keys, cache_values)
                ]
            )
            landed[mask] = exchange(block, "mp", mask) if mask else block
        caches = [landed[mask] for mask in masks]
    else:
        masks = [0]
        both = jnp.stack([cache_keys, cache_values]).reshape(
            2, seq_count, block_len, kv_heads, HD
        )
        to_all = jnp.repeat(jnp.moveaxis(both, 3, 0), model_size // kv_heads, axis=0)
        caches = [lax.all_to_all(to_all, "mp", 0, 0, tiled=True)]

    tables, rows = run(
        functools.partial(prepare_kernel, block_len, one_head_each, total, moves),
        [
            struct(STEPS, 2, seq_count, HD, dtype=f32),
            struct(5 + 2 * moves, seq_count, HD, dtype=jnp.int32),
        ],
        scalars,
        tables,
        scalars=1,
    )

    def load(*arrays, vmem):
        return run(
            load_kernel,
            [struct(*array.shape, dtype=array.dtype) for array in arrays],
            *arrays,
            copies=len(arrays),
            vmem=vmem,
            moved=sum(array.size * array.dtype.itemsize for array in arrays),
        )

    gain = norm_gain.reshape(1, width)
    w_key_value, hidden, gain = load(w_key_value, hidden_in, gain, vmem=COPY_VMEM)
    terms = ()
    fresh, kv_outputs = [], []
    for step in range(STEPS):
        made = run(
            functools.partial(norm_kernel, step, one_head_each),
            [struct(seq_count, width)] * (1 + (step > 0))
            + [struct(seq_count, col_width)]
            + [struct(seq_count, HD)] * (2 * one_head_each),
            rows,
            tables,
            gain,
            w_key_value,
            hidden,
            *terms,
        )
        if step > 0:
            hidden, *made = made
        normed, raw, *sent = made
        if one_head_each:
            kv_outputs.append(raw)
            pairs = model_size // 2
            to_even = [(low, 2 * low) for low in range(pairs)]
            to_odd = [(low, 2 * low + 1) for low in range(pairs)]
            fresh.append(
                lax.ppermute(sent[0], "mp", to_even + [(pairs + a, b) for a, b in to_odd])
            )
            fresh.append(
                lax.ppermute(sent[1], "mp", to_odd + [(pairs + a, b) for a, b in to_even])
            )
        else:
            raw_full = lax.all_gather(raw, "mp", axis=1, tiled=True)
            key_part = raw_full[:, :kv_width].astype(f32).reshape(seq_count, kv_heads, HD)
            key_part = root_norm(key_part)
            swapped = jnp.concatenate([key_part[..., half:], key_part[..., :half]], axis=-1)
            new_keys = (
                key_part * tables[step, 0][:, None, :] + swapped * tables[step, 1][:, None, :]
            ).astype(bf16)
            new_values = raw_full[:, kv_width:].reshape(seq_count, kv_heads, HD)
            live = (rows[0] > step)[:, None, :]
            new_kv = jnp.where(live, jnp.concatenate([new_keys, new_values], axis=1), 0)
            kv_outputs.append(
                lax.dynamic_slice_in_dim(
                    new_kv.reshape(seq_count, 2 * kv_width), model_index * col_width, col_width, 1
                )
            )
            fresh.append(lax.dynamic_index_in_dim(new_kv, own_head, 1, False))
            fresh.append(lax.dynamic_index_in_dim(new_kv, kv_heads + own_head, 1, False))
        if step == 0:
            w_query, w_output = load(w_query, w_output, vmem=LOAD_VMEM)
        sums = [struct(heads_here, seq_count, HD, dtype=f32)] * 4
        cost = {"flops": 2 * seq_count * width * heads_here * HD, "moved": 2 * width * heads_here * HD}
        if step > 0:
            attention = run(
                functools.partial(query_kernel, step, masks),
                sums,
                rows,
                tables,
                normed,
                w_query,
                *caches,
                vmem=KERNEL_VMEM,
                **cost,
            )
        else:
            queries = run(
                functools.partial(project_kernel, step),
                sums[0],
                tables,
                normed,
                w_query,
                vmem=KERNEL_VMEM,
                **cost,
            )
            attention = run(functools.partial(attend_kernel, masks), sums[1:], rows, queries, *caches)
            attention = [queries, *attention]
        part = run(
            output_kernel,
            struct(seq_count, width),
            rows,
            *attention,
            w_output,
            *fresh,
            vmem=KERNEL_VMEM,
        )
        terms = sum_rounds(part, "mp")

    own, sent = run(
        functools.partial(final_kernel, STEPS - 1),
        [struct(seq_count, width + STEPS * col_width), struct(moves, width + STEPS * col_width)],
        rows,
        hidden,
        *terms,
        *kv_outputs,
    )
    return tuple(
        run(
            trade_kernel,
            [struct(seq_count, width), struct(STEPS, seq_count, col_width)],
            rows,
            own,
            exchange(sent, "dp", 1),
        )
    )


def solution(mesh):
    placed = (
        P(("parts", "dp"), None),
        P(),
        P(None, "mp"),
        P(None, "mp"),
        P("mp", None),
        P(("parts", "dp"), "mp", None),
        P(("parts", "dp"), "mp", None),
        P("parts"),
        P("parts"),
        P("parts"),
        P("parts"),
    )
    return jax.shard_map(
        per_device,
        mesh=mesh,
        in_specs=placed,
        out_specs=(P(("parts", "dp"), None), P(None, ("parts", "dp"), "mp")),
        check_vma=False,
    )
```

```python
import functools
import math

import jax
import jax.numpy as jnp
from jax import lax
from jax.experimental import pallas as pl
from jax.experimental.pallas import tpu as pltpu
from jax.sharding import PartitionSpec as P

HD = 128
STEPS = 4
KERNEL_VMEM = 18 * 2**20
LOAD_VMEM = 28 * 2**20
COPY_VMEM = 8 * 2**20


rope_base = 1000000.0
norm_eps = 1e-06

in_vmem = pl.BlockSpec(memory_space=pltpu.VMEM)
in_smem = pl.BlockSpec(memory_space=pltpu.SMEM)
in_place = pl.BlockSpec(memory_space=pltpu.HBM)


def exchange(block, axis, mask):
    count = lax.axis_size(axis)
    return lax.ppermute(block, axis, [(low, low ^ mask) for low in range(count)])


def root_norm(values):
    return values * lax.rsqrt(jnp.mean(values * values, axis=-1, keepdims=True) + norm_eps)


def turn(values, cosine, sine):
    return values * cosine + pltpu.roll(values, values.shape[-1] // 2, 1) * sine


def prepare_kernel(block_len, one_head_each, total, moves, scalars_ref, tables_ref, tables_out, rows_out):
    me, group, count = scalars_ref[0], scalars_ref[1], scalars_ref[2]
    seq_count = rows_out.shape[1]
    first = pl.multiple_of(group * seq_count, seq_count)
    tables_out[...] = tables_ref[:, :, pl.ds(first, seq_count), :]
    rows = lax.broadcasted_iota(jnp.int32, rows_out.shape[1:], 0)

    def fill(value):
        return jnp.full(rows.shape, value, jnp.int32)

    remaining, lengths = fill(0), fill(0)
    for seq in range(seq_count):
        lengths = jnp.where(rows == seq, scalars_ref[3 + first + seq], lengths)
        remaining = jnp.where(rows == seq, scalars_ref[3 + total + first + seq], remaining)
    rows_out[0] = remaining
    rows_out[1] = lengths
    rows_out[2] = fill((2 * me < count).astype(jnp.int32))
    rows_out[3] = fill(((me & 1) == 0).astype(jnp.int32) if one_head_each else 1)
    rows_out[4] = fill(me * block_len if one_head_each else 0)
    for move in range(moves):
        slots = [scalars_ref[3 + 2 * total + moves * side + move] for side in range(2)]
        rows_out[5 + 2 * move] = fill(jnp.where(group == 0, slots[0], slots[1]))
        rows_out[6 + 2 * move] = fill(jnp.where(group == 0, slots[1], slots[0]))


def load_kernel(*refs):
    *refs, sems = refs
    count = len(refs) // 2
    copies = [
        pltpu.make_async_copy(source, target, sems.at[at])
        for at, (source, target) in enumerate(zip(refs[:count], refs[count:]))
    ]
    for copy in copies:
        copy.start()
    for copy in copies:
        copy.wait()


def updated(step, rows_ref, hidden_ref, first_ref, second_ref):
    hidden = hidden_ref[...].astype(jnp.float32)
    update = first_ref[...].astype(jnp.float32) + second_ref[...].astype(jnp.float32)
    return jnp.where(rows_ref[0][:, :1] > step, hidden + update, hidden)


def add_kernel(*refs):
    terms = [ref[...].astype(jnp.float32) for ref in refs[:-1]]
    while len(terms) > 1:
        terms = [one + other for one, other in zip(terms[0::2], terms[1::2])]
    refs[-1][...] = terms[0].astype(jnp.bfloat16)


def norm_kernel(step, split_heads, rows_ref, tables_ref, gain_ref, w_ref, *refs):
    if step > 0:
        hidden_ref, first_ref, second_ref, hidden_out, *refs = refs
        hidden = updated(step - 1, rows_ref, hidden_ref, first_ref, second_ref).astype(jnp.bfloat16)
        hidden_out[...] = hidden
        hidden = hidden.astype(jnp.float32)
    else:
        hidden_ref, *refs = refs
        hidden = hidden_ref[...].astype(jnp.float32)
    normed = (root_norm(hidden) * gain_ref[...]).astype(jnp.bfloat16)
    normed_out, raw_out, *refs = refs
    normed_out[...] = normed
    raw = jnp.dot(normed, w_ref[...], preferred_element_type=jnp.float32).astype(jnp.bfloat16)
    if not split_heads:
        raw_out[...] = raw
        return
    is_key = rows_ref[2] > 0
    live = rows_ref[0] > step
    done = []
    for head in range(2):
        piece = raw[:, head * HD : (head + 1) * HD].astype(jnp.float32)
        turned = turn(root_norm(piece), tables_ref[step, 0], tables_ref[step, 1])
        done.append(jnp.where(live, jnp.where(is_key, turned, piece), 0.0))
        raw_out[:, head * HD : (head + 1) * HD] = done[head].astype(jnp.bfloat16)
    a_out, b_out = refs
    a_out[...] = jnp.where(is_key, done[0], done[1]).astype(jnp.bfloat16)
    b_out[...] = jnp.where(is_key, done[1], done[0]).astype(jnp.bfloat16)


def project_kernel(step, tables_ref, normed_ref, w_ref, query_out):
    projected = jnp.dot(normed_ref[...], w_ref[...], preferred_element_type=jnp.float32)
    for head in range(query_out.shape[0]):
        piece = projected[:, head * HD : (head + 1) * HD]
        turned = turn(root_norm(piece), tables_ref[step, 0], tables_ref[step, 1])
        query_out[head] = turned.astype(jnp.bfloat16).astype(jnp.float32)


def query_kernel(step, masks, rows_ref, tables_ref, normed_ref, w_ref, *rest):
    *caches, query_out, num_out, max_out, den_out = rest
    project_kernel(step, tables_ref, normed_ref, w_ref, query_out)
    attend_kernel(masks, rows_ref, query_out, *caches, num_out, max_out, den_out)


def attend_kernel(masks, rows_ref, query_ref, *rest):
    *caches, num_out, max_out, den_out = rest
    caches = [cache for _, cache in sorted(zip(masks, caches), key=lambda pair: pair[0])]
    heads, seq_count = query_ref.shape[:2]

    def rows(which, seq):
        return jnp.concatenate(
            [
                ref[which, seq] if ref.ndim == 4 else ref[:, which, seq].reshape(-1, HD)
                for ref in caches
            ],
            axis=0,
        )

    scores = [
        lax.dot_general(
            query_ref[:, seq, :].astype(jnp.bfloat16),
            rows(0, seq),
            (((1,), (1,)), ((), ())),
            preferred_element_type=jnp.float32,
        )
        * (1.0 / math.sqrt(HD))
        for seq in range(seq_count)
    ]
    places = lax.broadcasted_iota(jnp.int32, scores[0].shape, 1) ^ rows_ref[4][:1, :1]
    lengths = rows_ref[1]
    valids = [places < lengths[seq : seq + 1, :1] for seq in range(seq_count)]
    tops = [
        jnp.max(jnp.where(valid, score, -1e30), axis=-1, keepdims=True)
        for valid, score in zip(valids, scores)
    ]
    weights = [
        jnp.where(valid, jnp.exp(score - top), 0.0).astype(jnp.bfloat16)
        for valid, score, top in zip(valids, scores, tops)
    ]
    for seq in range(seq_count):
        num_out[:, seq, :] = jnp.dot(
            weights[seq], rows(1, seq), preferred_element_type=jnp.float32
        )
        mass = jnp.sum(weights[seq].astype(jnp.float32), axis=-1, keepdims=True)
        max_out[:, seq, :] = jnp.broadcast_to(tops[seq], (heads, HD))
        den_out[:, seq, :] = jnp.broadcast_to(mass, (heads, HD))


def output_kernel(rows_ref, query_ref, num_ref, max_ref, den_ref, w_ref, *rest):
    fresh, out_ref = rest[:-1], rest[-1]
    heads = query_ref.shape[0]
    key_first = rows_ref[3] > 0
    keys, values = [], []
    for one_ref, other_ref in zip(fresh[0::2], fresh[1::2]):
        one, other = one_ref[...].astype(jnp.float32), other_ref[...].astype(jnp.float32)
        keys.append(jnp.where(key_first, one, other))
        values.append(jnp.where(key_first, other, one))
    attended = []
    for head in range(heads):
        query = query_ref[head]
        scores = [
            jnp.sum(query * key, axis=-1, keepdims=True) * (1.0 / math.sqrt(HD)) for key in keys
        ]
        top_old = max_ref[head]
        top = functools.reduce(jnp.maximum, scores, top_old)
        scale = jnp.exp(top_old - top)
        num = scale * num_ref[head]
        den = scale * den_ref[head]
        for score, value in zip(scores, values):
            weight = jnp.exp(score - top).astype(jnp.bfloat16).astype(jnp.float32)
            num = num + weight * value
            den = den + weight
        attended.append((num / den).astype(jnp.bfloat16))
    out_ref[...] = jnp.dot(
        jnp.concatenate(attended, axis=1), w_ref[...], preferred_element_type=jnp.float32
    ).astype(jnp.bfloat16)


def final_kernel(step, rows_ref, hidden_ref, first_ref, second_ref, *refs):
    *raws, out_ref, sent_ref = refs
    last = updated(step, rows_ref, hidden_ref, first_ref, second_ref).astype(jnp.bfloat16)
    own = jnp.concatenate([last] + [raw[...] for raw in raws], axis=1)
    out_ref[...] = own
    own = own.astype(jnp.float32)
    index = lax.broadcasted_iota(jnp.int32, own.shape, 0)
    moved = [
        jnp.sum(jnp.where(index == rows_ref[5 + 2 * move][:1, :1], own, 0.0), axis=0, keepdims=True)
        for move in range(sent_ref.shape[0])
    ]
    sent_ref[...] = jnp.concatenate(moved, axis=0).astype(jnp.bfloat16)


def trade_kernel(rows_ref, own_ref, got_ref, hidden_out, kv_out):
    own = own_ref[...].astype(jnp.float32)
    got = got_ref[...].astype(jnp.float32)
    index = lax.broadcasted_iota(jnp.int32, own.shape, 0)
    for move in range(got.shape[0]):
        own = jnp.where(index == rows_ref[5 + 2 * move][:1, :1], got[move : move + 1], own)
    own = own.astype(jnp.bfloat16)
    width = hidden_out.shape[1]
    hidden_out[...] = own[:, :width]
    for step in range(kv_out.shape[0]):
        columns = kv_out.shape[2]
        kv_out[step] = own[:, width + step * columns : width + (step + 1) * columns]


def run(kernel, outs, *args, scalars=0, copies=0, vmem=6 * 2**20, flops=0, moved=0):
    return pl.pallas_call(
        kernel,
        out_shape=outs,
        in_specs=[in_smem] * scalars + [in_place if copies else in_vmem] * (len(args) - scalars),
        out_specs=jax.tree.map(lambda _: in_vmem, outs),
        scratch_shapes=[pltpu.SemaphoreType.DMA((copies,))] if copies else [],
        cost_estimate=pl.CostEstimate(flops=flops, bytes_accessed=moved, transcendentals=0),
        compiler_params=pltpu.CompilerParams(vmem_limit_bytes=vmem),
    )(*args)


def sum_rounds(part, axis):
    masks = [1 << bit for bit in range(lax.axis_size(axis).bit_length() - 1)]
    *masks, last = masks
    while masks:
        now, masks = masks[:2], masks[2:]
        if len(now) == 2:
            now = now + [now[0] | now[1]]
        others = [exchange(part, axis, mask) for mask in now]
        part = run(
            add_kernel, jax.ShapeDtypeStruct(part.shape, part.dtype), *reversed(others), part
        )
    return part, exchange(part, axis, last)


def per_device(
    hidden_in,
    norm_gain,
    w_query,
    w_key_value,
    w_output,
    cache_keys,
    cache_values,
    cache_lengths,
    remaining_steps,
    move_from,
    move_to,
):
    bf16, f32 = jnp.bfloat16, jnp.float32
    seq_count, width = hidden_in.shape
    model_size = lax.axis_size("mp")
    model_index = lax.axis_index("mp")
    group_index = lax.axis_index("dp")
    heads_here = w_query.shape[1] // HD
    kv_width = cache_keys.shape[2]
    kv_heads = kv_width // HD
    block_len = cache_keys.shape[1]
    col_width = w_key_value.shape[1]
    one_head_each = model_size == kv_heads and col_width == 2 * HD

    def struct(*shape, dtype=bf16):
        return jax.ShapeDtypeStruct(shape, dtype)

    half = HD // 2
    frequency = rope_base ** (-(jnp.arange(HD) % half).astype(f32) * 2.0 / HD)
    positions = cache_lengths[None, :] + jnp.arange(STEPS)[:, None]
    angles = positions.astype(f32)[..., None] * frequency
    sign = jnp.where(jnp.arange(HD) < half, -1.0, 1.0)
    tables = jnp.stack([jnp.cos(angles), jnp.sin(angles) * sign], axis=1)
    total, moves = cache_lengths.shape[0], move_from.shape[0]
    place = jnp.stack([model_index, group_index, jnp.int32(model_size)])
    scalars = jnp.concatenate([place, cache_lengths, remaining_steps, move_from, move_to])
    own_head = model_index * kv_heads // model_size

    if one_head_each:
        half_size = model_size // 2
        across = list(range(half_size, model_size))
        within = list(range(1, half_size))
        masks = within + across + [0]
        landed = {}
        for mask in masks:
            head = (model_index ^ mask) * HD
            block = jnp.stack(
                [
                    lax.dynamic_slice_in_dim(cache, head, HD, 2)
                    for cache in (cache_keys, cache_values)
                ]
            )
            landed[mask] = exchange(block, "mp", mask) if mask else block
        caches = [landed[mask] for mask in masks]
    else:
        masks = [0]
        both = jnp.stack([cache_keys, cache_values]).reshape(
            2, seq_count, block_len, kv_heads, HD
        )
        to_all = jnp.repeat(jnp.moveaxis(both, 3, 0), model_size // kv_heads, axis=0)
        caches = [lax.all_to_all(to_all, "mp", 0, 0, tiled=True)]

    tables, rows = run(
        functools.partial(prepare_kernel, block_len, one_head_each, total, moves),
        [
            struct(STEPS, 2, seq_count, HD, dtype=f32),
            struct(5 + 2 * moves, seq_count, HD, dtype=jnp.int32),
        ],
        scalars,
        tables,
        scalars=1,
    )

    def load(*arrays, vmem):
        return run(
            load_kernel,
            [struct(*array.shape, dtype=array.dtype) for array in arrays],
            *arrays,
            copies=len(arrays),
            vmem=vmem,
            moved=sum(array.size * array.dtype.itemsize for array in arrays),
        )

    gain = norm_gain.reshape(1, width)
    w_key_value, hidden, gain = load(w_key_value, hidden_in, gain, vmem=COPY_VMEM)
    terms = ()
    fresh, kv_outputs = [], []
    for step in range(STEPS):
        made = run(
            functools.partial(norm_kernel, step, one_head_each),
            [struct(seq_count, width)] * (1 + (step > 0))
            + [struct(seq_count, col_width)]
            + [struct(seq_count, HD)] * (2 * one_head_each),
            rows,
            tables,
            gain,
            w_key_value,
            hidden,
            *terms,
        )
        if step > 0:
            hidden, *made = made
        normed, raw, *sent = made
        if one_head_each:
            kv_outputs.append(raw)
            pairs = model_size // 2
            to_even = [(low, 2 * low) for low in range(pairs)]
            to_odd = [(low, 2 * low + 1) for low in range(pairs)]
            fresh.append(
                lax.ppermute(sent[0], "mp", to_even + [(pairs + a, b) for a, b in to_odd])
            )
            fresh.append(
                lax.ppermute(sent[1], "mp", to_odd + [(pairs + a, b) for a, b in to_even])
            )
        else:
            raw_full = lax.all_gather(raw, "mp", axis=1, tiled=True)
            key_part = raw_full[:, :kv_width].astype(f32).reshape(seq_count, kv_heads, HD)
            key_part = root_norm(key_part)
            swapped = jnp.concatenate([key_part[..., half:], key_part[..., :half]], axis=-1)
            new_keys = (
                key_part * tables[step, 0][:, None, :] + swapped * tables[step, 1][:, None, :]
            ).astype(bf16)
            new_values = raw_full[:, kv_width:].reshape(seq_count, kv_heads, HD)
            live = (rows[0] > step)[:, None, :]
            new_kv = jnp.where(live, jnp.concatenate([new_keys, new_values], axis=1), 0)
            kv_outputs.append(
                lax.dynamic_slice_in_dim(
                    new_kv.reshape(seq_count, 2 * kv_width), model_index * col_width, col_width, 1
                )
            )
            fresh.append(lax.dynamic_index_in_dim(new_kv, own_head, 1, False))
            fresh.append(lax.dynamic_index_in_dim(new_kv, kv_heads + own_head, 1, False))
        if step == 0:
            w_query, w_output = load(w_query, w_output, vmem=LOAD_VMEM)
        sums = [struct(heads_here, seq_count, HD, dtype=f32)] * 4
        cost = {"flops": 2 * seq_count * width * heads_here * HD, "moved": 2 * width * heads_here * HD}
        if step > 0:
            attention = run(
                functools.partial(query_kernel, step, masks),
                sums,
                rows,
                tables,
                normed,
                w_query,
                *caches,
                vmem=KERNEL_VMEM,
                **cost,
            )
        else:
            queries = run(
                functools.partial(project_kernel, step),
                sums[0],
                tables,
                normed,
                w_query,
                vmem=KERNEL_VMEM,
                **cost,
            )
            attention = run(functools.partial(attend_kernel, masks), sums[1:], rows, queries, *caches)
            attention = [queries, *attention]
        part = run(
            output_kernel,
            struct(seq_count, width),
            rows,
            *attention,
            w_output,
            *fresh,
            vmem=KERNEL_VMEM,
        )
        terms = sum_rounds(part, "mp")

    own, sent = run(
        functools.partial(final_kernel, STEPS - 1),
        [struct(seq_count, width + STEPS * col_width), struct(moves, width + STEPS * col_width)],
        rows,
        hidden,
        *terms,
        *kv_outputs,
    )
    return tuple(
        run(
            trade_kernel,
            [struct(seq_count, width), struct(STEPS, seq_count, col_width)],
            rows,
            own,
            exchange(sent, "dp", 1),
        )
    )


def solution(mesh):
    placed = (
        P(("parts", "dp"), None),
        P(),
        P(None, "mp"),
        P(None, "mp"),
        P("mp", None),
        P(("parts", "dp"), "mp", None),
        P(("parts", "dp"), "mp", None),
        P("parts"),
        P("parts"),
        P("parts"),
        P("parts"),
    )
    return jax.shard_map(
        per_device,
        mesh=mesh,
        in_specs=placed,
        out_specs=(P(("parts", "dp"), None), P(None, ("parts", "dp"), "mp")),
        check_vma=False,
    )
```
